256 devices in a mesh: grp: 4 (over y), sub: 64 (over z, x, core).
Axes of the slice: x: 4, y: 4, z: 8, core: 2. Of those that a mesh axis runs over, the one named last changes fastest.
Arguments:
- model: float32 [2048, 64, 128], P('grp', 'sub'), may hold values from -4 to 4
- block_owner_rank: int32 [4, 32768, 8], P('grp', 'sub'), may hold values from 0 to 63, all different within a row; in each aligned block of 512 rows (0 to 511, 512 to 1023, ..., all dimensions but the last counted through in order) at most 128 rows name the same one
- source_slot: int32 [4, 32768, 8], P('grp', 'sub'), may hold values from 0 to 2047
- weights: float32 [4, 32768, 8], P('grp', 'sub'), may hold values from 0.05 to 0.3
- field: float32 [4, 2, 3, 512, 64, 128], P('grp', None, None, 'sub'), may hold values from -2 to 2
- source: float32 [4, 2, 3, 512, 64, 128], P('grp', None, None, 'sub'), may hold values from -6 to 6
- freq: float32 [4], P('grp'), may hold values from 0.5 to 4
Outputs:
- residual: float32 [4, 2, 3, 512, 64, 128], P('grp', None, None, 'sub')
The draws below stay inside these ranges and needn't reach their ends.
Inputs may be any that keep to these rules, and one draw needn't show every extreme that they name: `block_owner_rank`: each row names 8 different owners; among the rows of one subdomain's 512 columns (aligned blocks), no owner is named more than 128 times, a bound that some block reaches.
All inputs are finite; a program needn't handle non-finite values.
Results may differ from the reference program's by a relative error of at most 0.0003.
Values sent between devices are 32-bit elements; how exact they have to be, the bound alone decides.
No kernel may reach another device: no remote copies, remote signals or barrier semaphores. Data moves between devices by JAX's collectives and lax.ppermute only.
A program may use at most 192 MiB of HBM per device.

```python
import math
import jax
import jax.numpy as jnp
import numpy as np
from jax import lax

BLOCK = 128
K = 8
NY = 64
MESHES = 4
OWNERS = 64
SLOTS = 2048
CB_DEV = 512
CELL_BLOCKS = 32768
NX = 512
CAP = 128


def set_ends(array, own_key, low, high):
    extent = array.shape
    place = [jax.random.randint(jax.random.fold_in(own_key, axis), (), 0, extent[axis]) for axis in range(len(extent))]
    array = array.at[tuple(place)].set(low)
    longest = extent.index(max(extent))
    place[longest] = (place[longest] + 1) % extent[longest]
    return array.at[tuple(place)].set(high)


def level_of(stream_key, extent, split, smallest, high):
    def one(position, blocks):
        draws = jax.random.uniform(jax.random.fold_in(jax.random.fold_in(stream_key, 6), position), (blocks,), jnp.float32, smallest / len(split), high / len(split))
        return jnp.repeat(jnp.exp(draws), extent[position] // blocks).reshape((-1,) + (1,) * (len(extent) - position - 1))

    gain = one(*split[0])
    for cut in split[1:]:
        gain = gain * one(*cut)
    return gain


def shared_out(rng, own, number, rows, number_of, top, limit, skew):
    sequence = jax.random.permutation(rng, number_of)
    packed, common = load_shares(number_of, rows * top, limit, skew, True), load_shares(number_of, rows * top, limit, skew, False)
    places = jnp.arange(number_of)

    def named(tallies, offset_by):
        used = int((tallies > 0).sum())
        fixed = max(1, used // 4)
        shifted = fixed + (places - fixed + offset_by * (used - fixed)) % max(1, number_of - fixed)
        return jnp.zeros((number_of,), jnp.int32).at[sequence[jnp.where(places < fixed, places, shifted)]].set(jnp.asarray(tallies, jnp.int32))

    tallies = jnp.where(number % 4 == 0, named(packed, number // 4), named(common, number - number // 4 - 1))
    mixed = jax.random.permutation(jax.random.fold_in(own, 3), number_of)
    source_of, sink = mixed[0:number_of // 2 * 2:2], mixed[1:number_of // 2 * 2:2]
    slack = jnp.minimum(tallies[source_of] - 1, limit - tallies[sink]) // 2
    slack = jnp.where((source_of == sequence[0]) | (sink == sequence[0]) | (tallies[sink] == 0), 0, jnp.maximum(slack, 0))
    shifted = jax.random.randint(jax.random.fold_in(own, 4), (number_of // 2,), 0, 1 << 20) % (slack + 1)
    tallies = tallies.at[source_of].add(-shifted).at[sink].add(shifted)
    items = jnp.searchsorted(jnp.cumsum(tallies), jnp.arange(rows * top), side="right").astype(jnp.int32)
    listing = items.reshape(top, rows).T
    listing = listing[jax.random.permutation(jax.random.fold_in(own, 1), rows)]
    offset_by = jax.random.randint(jax.random.fold_in(own, 2), (rows, 1), 0, top)
    return jnp.take_along_axis(listing, (jnp.arange(top)[None, :] + offset_by) % top, axis=1)


def load_shares(amount, total, limit, slope, full):
    weights = [(1 << 20) // math.isqrt(grade ** slope) + 1 for grade in range(1, amount + 1)]
    largest = limit if full else min(limit, max(-(-total // amount), total * weights[0] // sum(weights)))
    least = 1 if total - largest >= amount - 1 else 0
    given, spare = [largest] + [least] * (amount - 1), total - largest - least * (amount - 1)
    while spare > 0:
        free = [i for i in range(1, amount) if given[i] < largest] or [i for i in range(1, amount) if given[i] < limit]
        pool, left = sum([weights[i] for i in free]), spare
        for i in free:
            extra = min(limit - given[i], max(1, left * weights[i] // pool), spare)
            given[i] = given[i] + extra
            spare = spare - extra
    return np.array(given)


def scatter_about(key, shape, scale, reach, shards=(), dtype=jnp.bfloat16):
    drawn = scale * jax.random.normal(key, shape, jnp.float32)
    if shards:
        drawn = drawn * level_of(key, shape, shards, -0.22, 0.18)
    return jnp.clip(drawn, -reach, reach).astype(dtype)


def setup_inputs(seed: int = 0) -> dict:
    splits = jax.random.split(jax.random.key(seed), 8)
    model = scatter_about(splits[0], (SLOTS, OWNERS, BLOCK), 0.8, 4.0, ((0, 4), (1, 64)), jnp.float32)
    block_owner_rank_keys = jax.random.split(jax.random.fold_in(splits[1], 1), MESHES * CELL_BLOCKS // CB_DEV)
    block_owner_rank_turns = jax.random.permutation(jax.random.fold_in(splits[1], 3), MESHES * CELL_BLOCKS // CB_DEV)
    block_owner_rank = jax.vmap(lambda own, number: shared_out(jax.random.fold_in(splits[1], 2), own, number, CB_DEV, OWNERS, K, CAP, 2))(block_owner_rank_keys, block_owner_rank_turns).reshape((MESHES, CELL_BLOCKS, K))
    source_slot = set_ends(jax.random.randint(splits[2], (MESHES, CELL_BLOCKS, K), 0, SLOTS), jax.random.fold_in(splits[2], 1), 0, SLOTS - 1).astype(jnp.int32)
    weights = jnp.clip(0.05 + 0.25 * jax.random.uniform(splits[3], (MESHES, CELL_BLOCKS, K), jnp.float32) ** level_of(splits[3], (MESHES, CELL_BLOCKS, K), ((0, 4), (1, 64)), -0.2, 0.2), 0.05, 0.3)
    field = scatter_about(splits[4], (MESHES, 2, 3, NX, NY, BLOCK), 0.25, 2.0, ((0, 4), (3, 64)), jnp.float32)
    source = scatter_about(splits[5], (MESHES, 2, 3, NX, NY, BLOCK), 1.0, 6.0, ((0, 4), (3, 64)), jnp.float32)
    freq = jnp.clip(jnp.exp(math.log(4.0) - 2.0794415 * jax.random.uniform(splits[6], (MESHES,), jnp.float32) ** level_of(splits[6], (MESHES,), ((0, 4),), -0.2, 0.2)), 0.5, 4.0)
    return dict(model=model, block_owner_rank=block_owner_rank, source_slot=source_slot, weights=weights, field=field, source=source, freq=freq)


def ahead(values, along):
    count = values.shape[along]
    tail = jnp.zeros_like(lax.slice_in_dim(values, 0, 1, axis=along))
    return jnp.concatenate([lax.slice_in_dim(values, 1, count, axis=along), tail], along)


def behind(values, along):
    count = values.shape[along]
    head = jnp.zeros_like(lax.slice_in_dim(values, 0, 1, axis=along))
    return jnp.concatenate([head, lax.slice_in_dim(values, 0, count - 1, axis=along)], along)


def lower_mean(values, along):
    count = values.shape[along]
    moved = jnp.concatenate([lax.slice_in_dim(values, 0, 1, axis=along), lax.slice_in_dim(values, 0, count - 1, axis=along)], along)
    return 0.5 * (values + moved)


def forward_diff(values, along):
    return ahead(values, along) - values


def backward_diff(values, along):
    return values - behind(values, along)


def curl_curl(efield):
    field_x, field_y, field_z = efield[:, 0], efield[:, 1], efield[:, 2]
    hx_part = forward_diff(field_z, 2) - forward_diff(field_y, 3)
    hy_part = forward_diff(field_x, 3) - forward_diff(field_z, 1)
    hz_part = forward_diff(field_y, 1) - forward_diff(field_x, 2)
    curl_x = backward_diff(hz_part, 2) - backward_diff(hy_part, 3)
    curl_y = backward_diff(hx_part, 3) - backward_diff(hz_part, 1)
    curl_z = backward_diff(hy_part, 1) - backward_diff(hx_part, 2)
    return jnp.stack([curl_x, curl_y, curl_z], 1)


def reference(model, block_owner_rank, source_slot, weights, field, source, freq):
    results = []
    for mesh_index in range(MESHES):
        selected_rows = model[source_slot[mesh_index], block_owner_rank[mesh_index]]
        log_cond = jnp.sum(weights[mesh_index][:, :, None] * selected_rows, axis=1).reshape(NX, NY, BLOCK)
        conduct = jnp.exp(log_cond)
        sig_x = lower_mean(lower_mean(conduct, 1), 2)
        sig_y = lower_mean(lower_mean(conduct, 2), 0)
        sig_z = lower_mean(lower_mean(conduct, 1), 0)
        sigma_edges = jnp.stack([sig_x, sig_y, sig_z], 0)
        efield = field[mesh_index]
        curl = curl_curl(efield)
        omega = freq[mesh_index]
        real_part = curl[0] - omega * sigma_edges * efield[1] - source[mesh_index, 0]
        imaginary_component = curl[1] + omega * sigma_edges * efield[0] - source[mesh_index, 1]
        results.append(jnp.stack([real_part, imaginary_component], 0))
    return jnp.stack(results, 0)
```

```python
import functools

import jax
import jax.numpy as jnp
from jax import lax
from jax.experimental import pallas as pl
from jax.experimental.pallas import tpu as pltpu
from jax.sharding import Mesh, PartitionSpec as P

CHUNK = 256
FIELDS = 3


def shift_of(count):
    return (count - 1).bit_length()


def lists_kernel(sizes, owner_ref, slot_ref, weight_ref, out_ref, values):
    nz, nx, nc, quarter, classes, cap = sizes
    top, columns = owner_ref.shape
    owner, slot, weight = owner_ref[...], slot_ref[...], weight_ref[...]
    bits_c, bits_x, bits_q = shift_of(nc), shift_of(nx), shift_of(quarter)
    kind = (slot >> bits_q) * nx + ((owner >> bits_c) & (nx - 1))
    row = ((owner >> (bits_c + bits_x)) * nc + (owner & (nc - 1))) * quarter + (slot & (quarter - 1))
    column = lax.broadcasted_iota(jnp.int32, (top, columns), 1)
    as_float = lambda value: value.astype(jnp.float32)
    rounded = lambda value: value.astype(jnp.bfloat16).astype(jnp.float32)
    high = rounded(weight)
    middle = rounded(weight - high)
    parts = [
        as_float(row >> 7),
        as_float(row & 127),
        as_float(column >> 8),
        as_float(column & 255),
        high,
        middle,
        weight - high - middle,
        jnp.ones((top, columns), jnp.float32),
    ]
    iota_kind = lax.broadcasted_iota(jnp.int32, (classes, columns), 0)
    marks = []
    for k in range(top):
        mark = iota_kind == kind[k : k + 1, :]
        marks.append(jnp.where(mark, 1.0, 0.0))
        stacked = [jnp.where(mark, part[k : k + 1, :], 0.0) for part in parts]
        values[k] = jnp.concatenate(stacked, 0).astype(jnp.bfloat16)
    marks = jnp.concatenate(marks, 0)
    marks_low = marks.astype(jnp.bfloat16)
    rows = top * classes
    before = lax.broadcasted_iota(jnp.int32, (columns, columns), 0) < lax.broadcasted_iota(
        jnp.int32, (columns, columns), 1
    )
    prefix = jnp.dot(
        marks_low,
        jnp.where(before, 1.0, 0.0).astype(jnp.bfloat16),
        preferred_element_type=jnp.float32,
    )
    row_i = lax.broadcasted_iota(jnp.int32, (rows, rows), 0)
    row_j = lax.broadcasted_iota(jnp.int32, (rows, rows), 1)
    earlier = (row_j < row_i) & ((row_i & (classes - 1)) == (row_j & (classes - 1)))
    above = jnp.dot(
        jnp.where(earlier, 1.0, 0.0).astype(jnp.bfloat16),
        marks_low,
        preferred_element_type=jnp.float32,
    )
    offset = jnp.sum(above, axis=1, keepdims=True)
    placed = marks * (prefix + offset)
    ranks = [
        jnp.sum(placed[k * classes : (k + 1) * classes], axis=0, keepdims=True).astype(jnp.int32)
        for k in range(top)
    ]
    totals = jnp.sum(marks, axis=1, keepdims=True)
    total = totals[:classes]
    for k in range(1, top):
        total = total + totals[k * classes : (k + 1) * classes]
    most = jnp.max(total.astype(jnp.int32))
    lane_rows = cap // 128
    spread = jnp.broadcast_to(total, (classes, 128))
    for c in range(classes):
        out_ref[c, FIELDS * lane_rows : FIELDS * lane_rows + 1, :] = spread[c : c + 1, :]
    iota_rank = lax.broadcasted_iota(jnp.int32, (CHUNK, columns), 0)

    def one_chunk(j, carry):
        found = jnp.zeros((CHUNK, len(parts) * classes), jnp.float32)
        for k in range(top):
            hot = jnp.where(iota_rank == ranks[k] - j * CHUNK, 1.0, 0.0).astype(jnp.bfloat16)
            found = found + lax.dot_general(
                hot, values[k], (((1,), (1,)), ((), ())), preferred_element_type=jnp.float32
            )
        turned = found.T
        part = lambda p: turned[p * classes : (p + 1) * classes]
        fields = [
            part(0) * 128.0 + part(1),
            part(4) + part(5) + part(6),
            part(2) * 256.0 + part(3) + part(7) - 1.0,
        ]
        for f in range(FIELDS):
            for h in range(CHUNK // 128):
                at = f * lane_rows + j * (CHUNK // 128) + h
                for c in range(classes):
                    out_ref[c, pl.ds(at, 1), :] = fields[f][c : c + 1, h * 128 : (h + 1) * 128]
        return carry

    lax.fori_loop(0, (most + CHUNK - 1) // CHUNK, one_chunk, 0)


def build_lists(sizes, owner, slot, weight):
    nz, nx, nc, quarter, classes, cap = sizes
    top, columns = owner.shape
    lane_rows = cap // 128
    return pl.pallas_call(
        functools.partial(lists_kernel, sizes),
        out_shape=jax.ShapeDtypeStruct((classes, FIELDS * lane_rows + 8, 128), jnp.float32),
        in_specs=[pl.BlockSpec(memory_space=pltpu.VMEM)] * 3,
        out_specs=pl.BlockSpec(memory_space=pltpu.VMEM),
        scratch_shapes=[pltpu.VMEM((top, 8 * classes, columns), jnp.bfloat16)],
        compiler_params=pltpu.CompilerParams(vmem_limit_bytes=24 * 1024 * 1024),
    )(owner, slot, weight)


STEP = 16


def partials_kernel(cap, where_ref, count_ref, row_ref, weight_ref, list_ref, table_ref, out_ref, picked):
    step = pl.program_id(0)
    columns = out_ref.shape[1]

    @pl.when(step == 0)
    def _():
        picked[...] = jnp.zeros_like(picked)

    count = count_ref[where_ref[step]]

    def gather(i, carry):
        base = pl.multiple_of(i * STEP, STEP)
        for u in range(STEP):
            picked[pl.ds(base + u, 1), :] = (
                table_ref[pl.ds(row_ref[0, 0, base + u], 1), :] * weight_ref[0, 0, base + u]
            )
        return carry

    lax.fori_loop(0, (count + STEP - 1) // STEP, gather, 0)
    out_ref[...] = jnp.zeros_like(out_ref)
    lane_rows = cap // 128
    iota = lax.broadcasted_iota(jnp.int32, (columns, 128), 0)

    def combine(j, carry):
        rows = picked[pl.ds(pl.multiple_of(j * CHUNK, CHUNK), CHUNK), :]
        high = rows.astype(jnp.bfloat16)
        low = (rows - high.astype(jnp.float32)).astype(jnp.bfloat16)
        both = jnp.concatenate([high, low], 1)
        hot = []
        for h in range(CHUNK // 128):
            at = 2 * lane_rows + j * (CHUNK // 128) + h
            place = list_ref[0, pl.ds(at, 1), :].astype(jnp.int32)
            hot.append(jnp.where(iota == place, 1.0, 0.0).astype(jnp.bfloat16))
        summed = jnp.dot(jnp.concatenate(hot, 1), both, preferred_element_type=jnp.float32)
        out_ref[0] += summed[:, :128] + summed[:, 128:]
        return carry

    lax.fori_loop(0, (count + CHUNK - 1) // CHUNK, combine, 0)


def partial_sums(cap, columns, order, counts, rows, weights, lists, table):
    steps = order.shape[0]
    places = rows.shape[0]
    return pl.pallas_call(
        functools.partial(partials_kernel, cap),
        grid_spec=pltpu.PrefetchScalarGridSpec(
            num_scalar_prefetch=2,
            grid=(steps,),
            in_specs=[
                pl.BlockSpec((1, 1, cap), lambda s, at, n: (at[s], 0, 0), memory_space=pltpu.SMEM),
                pl.BlockSpec((1, 1, cap), lambda s, at, n: (at[s], 0, 0), memory_space=pltpu.SMEM),
                pl.BlockSpec((1,) + lists.shape[1:], lambda s, at, n: (at[s], 0, 0)),
                pl.BlockSpec(table.shape, lambda s, at, n: (0, 0)),
            ],
            out_specs=pl.BlockSpec((1, columns, 128), lambda s, at, n: (s, 0, 0)),
            scratch_shapes=[pltpu.VMEM((cap, 128), jnp.float32)],
        ),
        out_shape=jax.ShapeDtypeStruct((steps, columns, 128), jnp.float32),
        compiler_params=pltpu.CompilerParams(vmem_limit_bytes=32 * 1024 * 1024),
    )(order, counts, rows, weights, lists, table)


def moved(value, axis, by):
    count = lax.axis_size(axis)
    return lax.ppermute(value, axis, [(i, (i + by) % count) for i in range(count)])


def ring_sum(get, axis):
    far = get(2)
    half = far.shape[0] // 2
    up = moved(far[:half], axis, 1)
    down = moved(far[half:], axis, -1)
    near_up, near_down = get(1), get(3)
    near_up = jnp.concatenate([near_up[:half] + up, near_up[half:]], 0)
    near_down = jnp.concatenate([near_down[:half], near_down[half:] + down], 0)
    return get(0) + moved(near_up, axis, 1) + moved(near_down, axis, -1)


def shifted(shard, axis, by):
    devices = lax.axis_size(axis)
    pairs = [(i, i + by) for i in range(devices) if 0 <= i + by < devices]
    return lax.ppermute(shard, axis, pairs)


def padded_2(shard, axis, dim, width):
    length = shard.shape[dim]
    last = lax.slice_in_dim(shard, length - width, length, axis=dim)
    initial = lax.slice_in_dim(shard, 0, width, axis=dim)
    before = shifted(last, axis, 1)
    after = shifted(initial, axis, -1)
    return jnp.concatenate([before, shard, after], axis=dim)


def ahead(values, along):
    count = values.shape[along]
    tail = jnp.zeros_like(lax.slice_in_dim(values, 0, 1, axis=along))
    return jnp.concatenate([lax.slice_in_dim(values, 1, count, axis=along), tail], along)


def behind(values, along):
    count = values.shape[along]
    head = jnp.zeros_like(lax.slice_in_dim(values, 0, 1, axis=along))
    return jnp.concatenate([head, lax.slice_in_dim(values, 0, count - 1, axis=along)], along)


def lower_mean(values, along):
    count = values.shape[along]
    before = jnp.concatenate(
        [
            lax.slice_in_dim(values, 0, 1, axis=along),
            lax.slice_in_dim(values, 0, count - 1, axis=along),
        ],
        along,
    )
    return 0.5 * (values + before)


def forward_diff(values, along):
    return ahead(values, along) - values


def backward_diff(values, along):
    return values - behind(values, along)


SUB = ("z", "x", "c")


def log_conductivity(model, block_owner_rank, source_slot, weights):
    ny, nz, nx, nc = (lax.axis_size(a) for a in ("y", "z", "x", "c"))
    quarter, block = model.shape[0], model.shape[2]
    columns, top = weights.shape[1:]
    table = lax.all_gather(model, ("z", "c"), axis=0, tiled=True).reshape(-1, block)
    classes = ny * nx
    cap = min(columns * top, nz * nc * 128)
    sizes = (nz, nx, nc, quarter, classes, cap)
    lists = build_lists(sizes, block_owner_rank[0].T, source_slot[0].T, weights[0].T)
    lists = lax.all_to_all(lists, ("y", "x"), split_axis=0, concat_axis=0, tiled=True)
    lane_rows = cap // 128
    rows = lists[:, :lane_rows].reshape(classes, 1, cap).astype(jnp.int32)
    factors = lists[:, lane_rows : 2 * lane_rows].reshape(classes, 1, cap)
    counts = lists[:, FIELDS * lane_rows, 0].astype(jnp.int32)
    step = jnp.arange(classes, dtype=jnp.int32)
    order = (lax.axis_index("y") + step // nx) % ny * nx + (lax.axis_index("x") + step % nx) % nx
    sums = partial_sums(cap, columns, order, counts, rows, factors, lists, table)
    sums = sums.reshape(ny, nx, columns, block)
    half = columns // 2
    first = ring_sum(lambda d: sums[d, :, :half], "y")
    second = ring_sum(lambda d: sums[:, d, half:], "x")
    first = sum((moved(first[d], "x", d) for d in (2, 1, 3)), first[0])
    second = sum((moved(second[d], "y", d) for d in (2, 1, 3)), second[0])
    return jnp.concatenate([first, second], 0)


def per_device(model, block_owner_rank, source_slot, weights, field, source, freq):
    efield = field[0]
    x_cell_count = efield.shape[2]
    cells_y = efield.shape[3]
    log_cond = log_conductivity(model, block_owner_rank, source_slot, weights)
    log_cond = log_cond.reshape(x_cell_count, cells_y, -1)
    conduct = jnp.exp(log_cond)
    first_device = lax.axis_index(SUB) == 0
    prior_plane = shifted(conduct[-1:], SUB, 1)
    prior_plane = jnp.where(first_device, conduct[:1], prior_plane)
    extended = jnp.concatenate([prior_plane, conduct], 0)
    sig_x = lower_mean(lower_mean(conduct, 1), 2)
    z_means = lower_mean(extended, 2)
    sig_y = 0.5 * (z_means[1:] + z_means[:-1])
    y_means = lower_mean(extended, 1)
    sig_z = 0.5 * (y_means[1:] + y_means[:-1])
    sigma_edges = jnp.stack([sig_x, sig_y, sig_z], 0)
    padded = padded_2(efield, SUB, 2, 1)
    field_x, field_y, field_z = (padded[:, 0], padded[:, 1], padded[:, 2])
    lower_x, lower_y, lower_z = (field_x[:, :-1], field_y[:, :-1], field_z[:, :-1])
    hx_part = forward_diff(lower_z, 2) - forward_diff(lower_y, 3)
    hy_part = forward_diff(lower_x, 3) - (field_z[:, 1:] - field_z[:, :-1])
    hz_part = field_y[:, 1:] - field_y[:, :-1] - forward_diff(lower_x, 2)
    rim_scale = jnp.where(first_device, 0.0, 1.0).astype(jnp.float32)
    plane_scale = jnp.concatenate(
        [rim_scale[None], jnp.ones((x_cell_count,), jnp.float32)]
    ).reshape(1, x_cell_count + 1, 1, 1)
    hx_part = hx_part * plane_scale
    hy_part = hy_part * plane_scale
    hz_part = hz_part * plane_scale
    curl_x = backward_diff(hz_part[:, 1:], 2) - backward_diff(hy_part[:, 1:], 3)
    curl_y = backward_diff(hx_part[:, 1:], 3) - (hz_part[:, 1:] - hz_part[:, :-1])
    curl_z = hy_part[:, 1:] - hy_part[:, :-1] - backward_diff(hx_part[:, 1:], 2)
    curl = jnp.stack([curl_x, curl_y, curl_z], 1)
    omega = freq[0]
    real_part = curl[0] - omega * sigma_edges * efield[1] - source[0, 0]
    imaginary_component = curl[1] + omega * sigma_edges * efield[0] - source[0, 1]
    return jnp.stack([real_part, imaginary_component], 0)[None]


def solution(mesh):
    fine = Mesh(mesh.devices.reshape(4, 8, 4, 2), ("y",) + SUB)
    in_specs = (
        P("y", SUB, None),
        P("y", SUB, None),
        P("y", SUB, None),
        P("y", SUB, None),
        P("y", None, None, SUB, None, None),
        P("y", None, None, SUB, None, None),
        P("y"),
    )
    out_specs = P("y", None, None, SUB, None, None)
    return jax.shard_map(
        per_device, mesh=fine, in_specs=in_specs, out_specs=out_specs, check_vma=False
    )
```

```python
import functools

import jax
import jax.numpy as jnp
from jax import lax
from jax.experimental import pallas as pl
from jax.experimental.pallas import tpu as pltpu
from jax.sharding import Mesh, PartitionSpec as P

CHUNK = 256
FIELDS = 3
STEP = 16
NEAR = 512


def shift_of(count):
    return (count - 1).bit_length()


def lists_kernel(sizes, owner_ref, slot_ref, weight_ref, out_ref, values):
    nz, nx, nc, quarter, classes, cap = sizes
    top, columns = owner_ref.shape
    owner, slot, weight = owner_ref[...], slot_ref[...], weight_ref[...]
    bits_c, bits_x, bits_q = shift_of(nc), shift_of(nx), shift_of(quarter)
    kind = (slot >> bits_q) * nx + ((owner >> bits_c) & (nx - 1))
    row = ((owner >> (bits_c + bits_x)) * nc + (owner & (nc - 1))) * quarter + (slot & (quarter - 1))
    column = lax.broadcasted_iota(jnp.int32, (top, columns), 1)
    as_float = lambda value: value.astype(jnp.float32)
    rounded = lambda value: value.astype(jnp.bfloat16).astype(jnp.float32)
    high = rounded(weight)
    middle = rounded(weight - high)
    parts = [
        as_float(row >> 7),
        as_float(row & 127),
        as_float(column >> 8),
        as_float(column & 255),
        high,
        middle,
        weight - high - middle,
        jnp.zeros((top, columns), jnp.float32),
    ]
    iota_kind = lax.broadcasted_iota(jnp.int32, (classes, columns), 0)
    marks = []
    for k in range(top):
        mark = iota_kind == kind[k : k + 1, :]
        marks.append(jnp.where(mark, 1.0, 0.0))
        stacked = [jnp.where(mark, part[k : k + 1, :], 0.0) for part in parts]
        values[k] = jnp.concatenate(stacked, 0).astype(jnp.bfloat16)
    marks = jnp.concatenate(marks, 0)
    marks_low = marks.astype(jnp.bfloat16)
    rows = top * classes
    half = columns // 2
    column_i = lax.broadcasted_iota(jnp.int32, (columns, columns), 0)
    column_j = lax.broadcasted_iota(jnp.int32, (columns, columns), 1)
    before = (column_i < column_j) & ((column_i >= half) == (column_j >= half))
    prefix = jnp.dot(
        marks_low,
        jnp.where(before, 1.0, 0.0).astype(jnp.bfloat16),
        preferred_element_type=jnp.float32,
    )
    row_i = lax.broadcasted_iota(jnp.int32, (rows, rows), 0)
    row_j = lax.broadcasted_iota(jnp.int32, (rows, rows), 1)
    earlier = (row_j < row_i) & ((row_i & (classes - 1)) == (row_j & (classes - 1)))
    above = jnp.dot(
        jnp.where(earlier, 1.0, 0.0).astype(jnp.bfloat16),
        marks_low,
        preferred_element_type=jnp.float32,
    )
    over = lambda value: jnp.sum(value, axis=1, keepdims=True)

    def per_kind(value):
        sums = over(value)
        total = sums[:classes]
        for k in range(1, top):
            total = total + sums[k * classes : (k + 1) * classes]
        return total

    count_a, count_b = per_kind(marks[:, :half]), per_kind(marks[:, half:])
    begin_b = ((count_a.astype(jnp.int32) + 127) >> 7) << 7
    most = jnp.max(begin_b + count_b.astype(jnp.int32))
    begin_rows = jnp.concatenate([begin_b.astype(jnp.float32)] * top, 0)
    base_a, base_b = over(above[:, :half]), over(above[:, half:]) + begin_rows
    lanes = lax.broadcasted_iota(jnp.int32, (rows, columns), 1)
    placed = marks * (prefix + jnp.where(lanes < half, base_a, base_b))
    ranks = [
        jnp.sum(placed[k * classes : (k + 1) * classes], axis=0, keepdims=True).astype(jnp.int32)
        for k in range(top)
    ]
    lane_rows = cap // 128
    for f, total in enumerate((count_a, count_b)):
        spread = jnp.broadcast_to(total, (classes, 128))
        for c in range(classes):
            at = FIELDS * lane_rows + f
            out_ref[c, at : at + 1, :] = spread[c : c + 1, :]
    iota_rank = lax.broadcasted_iota(jnp.int32, (CHUNK, columns), 0)

    def one_chunk(j, carry):
        found = jnp.zeros((CHUNK, len(parts) * classes), jnp.float32)
        for k in range(top):
            hot = jnp.where(iota_rank == ranks[k] - j * CHUNK, 1.0, 0.0).astype(jnp.bfloat16)
            found = found + lax.dot_general(
                hot, values[k], (((1,), (1,)), ((), ())), preferred_element_type=jnp.float32
            )
        turned = found.T
        part = lambda p: turned[p * classes : (p + 1) * classes]
        fields = [
            part(0) * 128.0 + part(1),
            part(4) + part(5) + part(6),
            part(2) * 256.0 + part(3),
        ]
        for f in range(FIELDS):
            for h in range(CHUNK // 128):
                at = f * lane_rows + j * (CHUNK // 128) + h
                for c in range(classes):
                    out_ref[c, pl.ds(at, 1), :] = fields[f][c : c + 1, h * 128 : (h + 1) * 128]
        return carry

    lax.fori_loop(0, (most + CHUNK - 1) // CHUNK, one_chunk, 0)


def build_lists(sizes, owner, slot, weight):
    nz, nx, nc, quarter, classes, cap = sizes
    top, columns = owner.shape
    lane_rows = cap // 128
    return pl.pallas_call(
        functools.partial(lists_kernel, sizes),
        out_shape=jax.ShapeDtypeStruct((classes, -(-(FIELDS * lane_rows + 2) // 8) * 8, 128), jnp.float32),
        in_specs=[pl.BlockSpec(memory_space=pltpu.VMEM)] * 3,
        out_specs=pl.BlockSpec(memory_space=pltpu.VMEM),
        scratch_shapes=[pltpu.VMEM((top, 8 * classes, columns), jnp.bfloat16)],
        compiler_params=pltpu.CompilerParams(vmem_limit_bytes=24 * 1024 * 1024),
    )(owner, slot, weight)


def partials_kernel(
    jobs, sizes, place_ref, count_ref, row_ref, weight_ref, rows_far, weights_far, list_ref, table_ref, *rest
):
    ny, nx, cap = sizes
    outs, (picked, row_chunk, weight_chunk, sems) = rest[: len(jobs)], rest[len(jobs) :]
    columns = outs[0].shape[1]
    lane_rows = cap // 128
    iota = lax.broadcasted_iota(jnp.int32, (columns, 128), 0)
    lanes = lax.broadcasted_iota(jnp.int32, (1, 128), 1)
    picked[...] = jnp.zeros_like(picked)

    def gather(rows, weights, first, count):
        def some(i, carry):
            base = pl.multiple_of(i * STEP, STEP)
            for u in range(STEP):
                picked[pl.ds(base + u, 1), :] = (
                    table_ref[pl.ds(rows[first + base + u], 1), :] * weights[first + base + u]
                )
            return carry

        lax.fori_loop(0, (count + STEP - 1) // STEP, some, 0)

    def chunk_sum(half, at, begin, count, j):
        first = begin + j * CHUNK
        left = jnp.minimum(count - j * CHUNK, CHUNK)
        near = first + CHUNK <= NEAR

        @pl.when(near)
        def _():
            gather(row_ref, weight_ref, at * NEAR + first, left)

        @pl.when(jnp.logical_not(near))
        def _():
            span = pl.ds(pl.multiple_of(first, 128), CHUNK)
            one = pltpu.make_async_copy(rows_far.at[at, 0, span], row_chunk, sems.at[0])
            two = pltpu.make_async_copy(weights_far.at[at, 0, span], weight_chunk, sems.at[1])
            one.start()
            two.start()
            one.wait()
            two.wait()
            gather(row_chunk, weight_chunk, 0, left)

        rows = picked[...]
        high = rows.astype(jnp.bfloat16)
        low = (rows - high.astype(jnp.float32)).astype(jnp.bfloat16)
        hot = []
        for h in range(CHUNK // 128):
            line = 2 * lane_rows + lax.shift_right_logical(first, 7) + h
            place = list_ref[at, pl.ds(line, 1), :].astype(jnp.int32) - half * columns
            place = jnp.where(lanes < left - h * 128, place, -1)
            hot.append(jnp.where(iota == place, 1.0, 0.0).astype(jnp.bfloat16))
        summed = jnp.dot(
            jnp.concatenate(hot, 1), jnp.concatenate([high, low], 1), preferred_element_type=jnp.float32
        )
        return summed[:, :128] + summed[:, 128:]

    for (half, dy, dx), out_ref in zip(jobs, outs):

        def one(t, carry):
            y = (place_ref[0] + (t if dy is None else dy)) % ny
            x = (place_ref[1] + (t if dx is None else dx)) % nx
            at = y * nx + x
            count_a = count_ref[at]
            count = count_ref[ny * nx + at] if half else count_a
            begin = lax.shift_left(lax.shift_right_logical(count_a + 127, 7), 7) if half else 0
            out_ref[t] = chunk_sum(half, at, begin, count, 0)

            def more(j, carry):
                out_ref[t] += chunk_sum(half, at, begin, count, j)
                return carry

            lax.fori_loop(1, (count + CHUNK - 1) // CHUNK, more, 0)
            return carry

        lax.fori_loop(0, out_ref.shape[0], one, 0)


def partial_sums(jobs, sizes, half, place, counts, near_rows, near_weights, rows, weights, lists, table):
    ny, nx, cap = sizes
    vmem = pl.BlockSpec(memory_space=pltpu.VMEM)
    smem = pl.BlockSpec(memory_space=pltpu.SMEM)
    anywhere = pl.BlockSpec(memory_space=pl.ANY)
    return pl.pallas_call(
        functools.partial(partials_kernel, jobs, sizes),
        in_specs=[smem, smem, smem, smem, anywhere, anywhere, vmem, vmem],
        out_specs=[vmem] * len(jobs),
        scratch_shapes=[
            pltpu.VMEM((CHUNK, 128), jnp.float32),
            pltpu.SMEM((CHUNK,), jnp.int32),
            pltpu.SMEM((CHUNK,), jnp.float32),
            pltpu.SemaphoreType.DMA((2,)),
        ],
        out_shape=[
            jax.ShapeDtypeStruct((nx if dx is None else ny, half, 128), jnp.float32)
            for _, dy, dx in jobs
        ],
        compiler_params=pltpu.CompilerParams(vmem_limit_bytes=24 * 1024 * 1024),
        cost_estimate=pl.CostEstimate(
            flops=0, bytes_accessed=len(jobs) * 5 * 1024 * 1024, transcendentals=0
        ),
    )(place, counts, near_rows, near_weights, rows, weights, lists, table)


def moved(value, axis, by):
    count = lax.axis_size(axis)
    return lax.ppermute(value, axis, [(i, (i + by) % count) for i in range(count)])


def shifted(shard, axis, by):
    devices = lax.axis_size(axis)
    pairs = [(i, i + by) for i in range(devices) if 0 <= i + by < devices]
    return lax.ppermute(shard, axis, pairs)


def padded_2(shard, axis, dim, width):
    length = shard.shape[dim]
    last = lax.slice_in_dim(shard, length - width, length, axis=dim)
    initial = lax.slice_in_dim(shard, 0, width, axis=dim)
    before = shifted(last, axis, 1)
    after = shifted(initial, axis, -1)
    return jnp.concatenate([before, shard, after], axis=dim)


def ahead(values, along):
    count = values.shape[along]
    tail = jnp.zeros_like(lax.slice_in_dim(values, 0, 1, axis=along))
    return jnp.concatenate([lax.slice_in_dim(values, 1, count, axis=along), tail], along)


def behind(values, along):
    count = values.shape[along]
    head = jnp.zeros_like(lax.slice_in_dim(values, 0, 1, axis=along))
    return jnp.concatenate([head, lax.slice_in_dim(values, 0, count - 1, axis=along)], along)


def lower_mean(values, along):
    count = values.shape[along]
    before = jnp.concatenate(
        [
            lax.slice_in_dim(values, 0, 1, axis=along),
            lax.slice_in_dim(values, 0, count - 1, axis=along),
        ],
        along,
    )
    return 0.5 * (values + before)


def forward_diff(values, along):
    return ahead(values, along) - values


def backward_diff(values, along):
    return values - behind(values, along)


SUB = ("z", "x", "c")


def log_conductivity(model, block_owner_rank, source_slot, weights):
    ny, nz, nx, nc = (lax.axis_size(a) for a in ("y", "z", "x", "c"))
    quarter, block = model.shape[0], model.shape[2]
    columns, top = weights.shape[1:]
    table = lax.all_gather(model, ("z", "c"), axis=0, tiled=True).reshape(-1, block)
    classes = ny * nx
    cap = min(columns * top, nz * nc * 128) + CHUNK
    sizes = (nz, nx, nc, quarter, classes, cap)
    lists = build_lists(sizes, block_owner_rank[0].T, source_slot[0].T, weights[0].T)
    lists = lax.all_to_all(lists, ("y", "x"), split_axis=0, concat_axis=0, tiled=True)
    lane_rows, near = cap // 128, NEAR // 128
    rows = lists[:, :lane_rows].reshape(classes, 1, cap).astype(jnp.int32)
    factors = lists[:, lane_rows : 2 * lane_rows].reshape(classes, 1, cap)
    near_rows = lists[:, :near].reshape(-1).astype(jnp.int32)
    near_factors = lists[:, lane_rows : lane_rows + near].reshape(-1)
    counts = lists[:, FIELDS * lane_rows : FIELDS * lane_rows + 2, 0].T.reshape(-1).astype(jnp.int32)
    place = jnp.stack([lax.axis_index("y"), lax.axis_index("x")]).astype(jnp.int32)

    def sums(*jobs):
        return partial_sums(
            jobs, (ny, nx, cap), columns // 2, place, counts, near_rows, near_factors, rows, factors, lists, table
        )

    a2, b2 = sums((0, 2, None), (1, None, 2))
    a1, a3, b1, b3 = sums((0, 1, None), (0, 3, None), (1, None, 1), (1, None, 3))
    a0, b0 = sums((0, 0, None), (1, None, 0))
    from_a = [moved(a2, "y", 2), moved(a1, "y", 1), moved(a3, "y", 3)]
    from_b = [moved(b2, "x", 2), moved(b1, "x", 1), moved(b3, "x", 3)]
    first = [a0[d] + from_a[0][d] + from_a[1][d] + from_a[2][d] for d in range(nx)]
    second = [b0[d] + from_b[0][d] + from_b[1][d] + from_b[2][d] for d in range(ny)]
    first = sum((moved(first[d], "x", d) for d in (2, 1, 3)), first[0])
    second = sum((moved(second[d], "y", d) for d in (2, 1, 3)), second[0])
    return jnp.concatenate([first, second], 0)


def per_device(model, block_owner_rank, source_slot, weights, field, source, freq):
    efield = field[0]
    x_cell_count = efield.shape[2]
    cells_y = efield.shape[3]
    log_cond = log_conductivity(model, block_owner_rank, source_slot, weights)
    log_cond = log_cond.reshape(x_cell_count, cells_y, -1)
    conduct = jnp.exp(log_cond)
    first_device = lax.axis_index(SUB) == 0
    prior_plane = shifted(conduct[-1:], SUB, 1)
    prior_plane = jnp.where(first_device, conduct[:1], prior_plane)
    extended = jnp.concatenate([prior_plane, conduct], 0)
    sig_x = lower_mean(lower_mean(conduct, 1), 2)
    z_means = lower_mean(extended, 2)
    sig_y = 0.5 * (z_means[1:] + z_means[:-1])
    y_means = lower_mean(extended, 1)
    sig_z = 0.5 * (y_means[1:] + y_means[:-1])
    sigma_edges = jnp.stack([sig_x, sig_y, sig_z], 0)
    padded = padded_2(efield, SUB, 2, 1)
    field_x, field_y, field_z = (padded[:, 0], padded[:, 1], padded[:, 2])
    lower_x, lower_y, lower_z = (field_x[:, :-1], field_y[:, :-1], field_z[:, :-1])
    hx_part = forward_diff(lower_z, 2) - forward_diff(lower_y, 3)
    hy_part = forward_diff(lower_x, 3) - (field_z[:, 1:] - field_z[:, :-1])
    hz_part = field_y[:, 1:] - field_y[:, :-1] - forward_diff(lower_x, 2)
    rim_scale = jnp.where(first_device, 0.0, 1.0).astype(jnp.float32)
    plane_scale = jnp.concatenate(
        [rim_scale[None], jnp.ones((x_cell_count,), jnp.float32)]
    ).reshape(1, x_cell_count + 1, 1, 1)
    hx_part = hx_part * plane_scale
    hy_part = hy_part * plane_scale
    hz_part = hz_part * plane_scale
    curl_x = backward_diff(hz_part[:, 1:], 2) - backward_diff(hy_part[:, 1:], 3)
    curl_y = backward_diff(hx_part[:, 1:], 3) - (hz_part[:, 1:] - hz_part[:, :-1])
    curl_z = hy_part[:, 1:] - hy_part[:, :-1] - backward_diff(hx_part[:, 1:], 2)
    curl = jnp.stack([curl_x, curl_y, curl_z], 1)
    omega = freq[0]
    real_part = curl[0] - omega * sigma_edges * efield[1] - source[0, 0]
    imaginary_component = curl[1] + omega * sigma_edges * efield[0] - source[0, 1]
    return jnp.stack([real_part, imaginary_component], 0)[None]


def solution(mesh):
    fine = Mesh(mesh.devices.reshape(4, 8, 4, 2), ("y",) + SUB)
    in_specs = (
        P("y", SUB, None),
        P("y", SUB, None),
        P("y", SUB, None),
        P("y", SUB, None),
        P("y", None, None, SUB, None, None),
        P("y", None, None, SUB, None, None),
        P("y"),
    )
    out_specs = P("y", None, None, SUB, None, None)
    return jax.shard_map(
        per_device, mesh=fine, in_specs=in_specs, out_specs=out_specs, check_vma=False
    )
```

```python
import functools

import jax
import jax.numpy as jnp
from jax import lax
from jax.experimental import pallas as pl
from jax.experimental.pallas import tpu as pltpu
from jax.sharding import Mesh, PartitionSpec as P

CHUNK = 256
FIELDS = 3
STEP = 16
NEAR = 512


def shift_of(count):
    return (count - 1).bit_length()


def lists_kernel(sizes, here_ref, owner_far, slot_far, weight_far, after_ref, out_ref, values, *rest):
    nz, nx, nc, quarter, classes, cap = sizes
    top, columns = owner_far.shape
    owner_ref, slot_ref, weight_ref, sems = rest
    copies = [
        pltpu.make_async_copy(far, near, sems.at[i])
        for i, (far, near) in enumerate(
            ((owner_far, owner_ref), (slot_far, slot_ref), (weight_far, weight_ref))
        )
    ]
    for copy in copies:
        copy.start()
    for copy in copies:
        copy.wait()
    owner, slot, weight = owner_ref[...], slot_ref[...], weight_ref[...]
    bits_c, bits_x, bits_q = shift_of(nc), shift_of(nx), shift_of(quarter)
    kind = (slot >> bits_q) * nx + ((owner >> bits_c) & (nx - 1))
    layer = (((owner >> (bits_c + bits_x)) - here_ref[0]) * (2 * here_ref[1] - 1)) & (nz - 1)
    core = (owner - here_ref[1]) & (nc - 1)
    row = (core * nz + layer) * quarter + (slot & (quarter - 1))
    column = lax.broadcasted_iota(jnp.int32, (top, columns), 1)
    as_float = lambda value: value.astype(jnp.float32)
    rounded = lambda value: value.astype(jnp.bfloat16).astype(jnp.float32)
    high = rounded(weight)
    middle = rounded(weight - high)
    parts = [
        as_float(row >> 7),
        as_float(row & 127),
        as_float(column >> 8),
        as_float(column & 255),
        high,
        middle,
        weight - high - middle,
        jnp.zeros((top, columns), jnp.float32),
    ]
    iota_kind = lax.broadcasted_iota(jnp.int32, (classes, columns), 0)
    marks = []
    for k in range(top):
        mark = iota_kind == kind[k : k + 1, :]
        marks.append(jnp.where(mark, 1.0, 0.0))
        stacked = [jnp.where(mark, part[k : k + 1, :], 0.0) for part in parts]
        values[k] = jnp.concatenate(stacked, 0).astype(jnp.bfloat16)
    marks = jnp.concatenate(marks, 0)
    marks_low = marks.astype(jnp.bfloat16)
    rows = top * classes
    half = columns // 2
    column_i = lax.broadcasted_iota(jnp.int32, (columns, columns), 0)
    column_j = lax.broadcasted_iota(jnp.int32, (columns, columns), 1)
    before = (column_i < column_j) & ((column_i >= half) == (column_j >= half))
    prefix = jnp.dot(
        marks_low,
        jnp.where(before, 1.0, 0.0).astype(jnp.bfloat16),
        preferred_element_type=jnp.float32,
    )
    row_i = lax.broadcasted_iota(jnp.int32, (rows, rows), 0)
    row_j = lax.broadcasted_iota(jnp.int32, (rows, rows), 1)
    earlier = (row_j < row_i) & ((row_i & (classes - 1)) == (row_j & (classes - 1)))
    above = jnp.dot(
        jnp.where(earlier, 1.0, 0.0).astype(jnp.bfloat16),
        marks_low,
        preferred_element_type=jnp.float32,
    )
    over = lambda value: jnp.sum(value, axis=1, keepdims=True)

    def per_kind(value):
        sums = over(value)
        total = sums[:classes]
        for k in range(1, top):
            total = total + sums[k * classes : (k + 1) * classes]
        return total

    count_a, count_b = per_kind(marks[:, :half]), per_kind(marks[:, half:])
    begin_b = ((count_a.astype(jnp.int32) + 127) >> 7) << 7
    most = jnp.max(begin_b + count_b.astype(jnp.int32))
    begin_rows = jnp.concatenate([begin_b.astype(jnp.float32)] * top, 0)
    base_a, base_b = over(above[:, :half]), over(above[:, half:]) + begin_rows
    lanes = lax.broadcasted_iota(jnp.int32, (rows, columns), 1)
    placed = marks * (prefix + jnp.where(lanes < half, base_a, base_b))
    ranks = [
        jnp.sum(placed[k * classes : (k + 1) * classes], axis=0, keepdims=True).astype(jnp.int32)
        for k in range(top)
    ]
    lane_rows = cap // 128
    for f, total in enumerate((count_a, count_b)):
        spread = jnp.broadcast_to(total, (classes, 128))
        for c in range(classes):
            at = FIELDS * lane_rows + f
            out_ref[c, at : at + 1, :] = spread[c : c + 1, :]
    iota_rank = lax.broadcasted_iota(jnp.int32, (CHUNK, columns), 0)

    def one_chunk(j, carry):
        found = jnp.zeros((CHUNK, len(parts) * classes), jnp.float32)
        for k in range(top):
            hot = jnp.where(iota_rank == ranks[k] - j * CHUNK, 1.0, 0.0).astype(jnp.bfloat16)
            found = found + lax.dot_general(
                hot, values[k], (((1,), (1,)), ((), ())), preferred_element_type=jnp.float32
            )
        turned = found.T
        part = lambda p: turned[p * classes : (p + 1) * classes]
        fields = [
            part(0) * 128.0 + part(1),
            part(4) + part(5) + part(6),
            part(2) * 256.0 + part(3),
        ]
        for f in range(FIELDS):
            for h in range(CHUNK // 128):
                at = f * lane_rows + j * (CHUNK // 128) + h
                for c in range(classes):
                    out_ref[c, pl.ds(at, 1), :] = fields[f][c : c + 1, h * 128 : (h + 1) * 128]
        return carry

    lax.fori_loop(0, (most + CHUNK - 1) // CHUNK, one_chunk, 0)


def build_lists(sizes, here, owner, slot, weight, after):
    nz, nx, nc, quarter, classes, cap = sizes
    top, columns = owner.shape
    lane_rows = cap // 128
    return pl.pallas_call(
        functools.partial(lists_kernel, sizes),
        out_shape=jax.ShapeDtypeStruct((classes, -(-(FIELDS * lane_rows + 2) // 8) * 8, 128), jnp.float32),
        in_specs=[pl.BlockSpec(memory_space=pltpu.SMEM)] + [pl.BlockSpec(memory_space=pl.ANY)] * 4,
        out_specs=pl.BlockSpec(memory_space=pltpu.VMEM),
        scratch_shapes=[
            pltpu.VMEM((top, 8 * classes, columns), jnp.bfloat16),
            pltpu.VMEM((top, columns), jnp.int32),
            pltpu.VMEM((top, columns), jnp.int32),
            pltpu.VMEM((top, columns), jnp.float32),
            pltpu.SemaphoreType.DMA((3,)),
        ],
        cost_estimate=pl.CostEstimate(flops=0, bytes_accessed=12 * 1024 * 1024, transcendentals=0),
        compiler_params=pltpu.CompilerParams(vmem_limit_bytes=24 * 1024 * 1024),
    )(here, owner, slot, weight, after)


def partials_kernel(
    jobs, sizes, place_ref, count_ref, row_ref, weight_ref, list_ref, table_ref, after_ref, *rest
):
    ny, nx, cap = sizes
    outs, (picked,) = rest[: len(jobs)], rest[len(jobs) :]
    columns = outs[0].shape[1] // 2
    lane_rows = cap // 128
    iota = lax.broadcasted_iota(jnp.int32, (columns, 128), 0)
    lanes = lax.broadcasted_iota(jnp.int32, (1, 128), 1)
    picked[...] = jnp.zeros_like(picked)

    def gather(rows, weights, first, count):
        def some(i, carry):
            base = pl.multiple_of(i * STEP, STEP)
            for u in range(STEP):
                picked[pl.ds(base + u, 1), :] = (
                    table_ref[pl.ds(rows[first + base + u], 1), :] * weights[first + base + u]
                )
            return carry

        lax.fori_loop(0, (count + STEP - 1) // STEP, some, 0)

    def chunk_sum(half, at, begin, count, j):
        first = begin + j * CHUNK
        left = jnp.minimum(count - j * CHUNK, CHUNK)
        near = first + CHUNK <= NEAR

        @pl.when(near)
        def _():
            gather(row_ref, weight_ref, at * NEAR + first, left)

        @pl.when(jnp.logical_not(near))
        def _():
            def single(u, carry):
                line = lax.shift_right_logical(first + u, 7)
                here = lanes == jnp.bitwise_and(first + u, 127)
                pick = lambda f: jnp.sum(
                    jnp.where(here, list_ref[at, pl.ds(f * lane_rows + line, 1), :], 0.0)
                )
                row = pick(0).astype(jnp.int32)
                picked[pl.ds(u, 1), :] = table_ref[pl.ds(row, 1), :] * pick(1)
                return carry

            lax.fori_loop(0, left, single, 0)

        rows = picked[...]
        high = rows.astype(jnp.bfloat16)
        low = (rows - high.astype(jnp.float32)).astype(jnp.bfloat16)
        hot = []
        for h in range(CHUNK // 128):
            line = 2 * lane_rows + lax.shift_right_logical(first, 7) + h
            place = list_ref[at, pl.ds(line, 1), :].astype(jnp.int32) - half * columns
            place = jnp.where(lanes < left - h * 128, place, -1)
            hot.append(jnp.where(iota == place, 1.0, 0.0).astype(jnp.bfloat16))
        summed = jnp.dot(
            jnp.concatenate(hot, 1), jnp.concatenate([high, low], 1), preferred_element_type=jnp.float32
        )
        return summed[:, :128] + summed[:, 128:]

    for offset, out_ref in zip(jobs, outs):

        def one(t, carry):
            swap = place_ref[2]
            y = (place_ref[0] + jnp.where(swap == 0, offset, t)) % ny
            x = (place_ref[1] + jnp.where(swap == 0, t, offset)) % nx
            at = y * nx + x
            count_a = count_ref[at]
            begin_b = lax.shift_left(lax.shift_right_logical(count_a + 127, 7), 7)
            for half, count, begin in ((0, count_a, 0), (1, count_ref[ny * nx + at], begin_b)):
                span = pl.ds(half * columns, columns)
                out_ref[t, span, :] = chunk_sum(half, at, begin, count, 0)

                def more(j, carry):
                    out_ref[t, span, :] += chunk_sum(half, at, begin, count, j)
                    return carry

                lax.fori_loop(1, (count + CHUNK - 1) // CHUNK, more, 0)
            return carry

        lax.fori_loop(0, out_ref.shape[0], one, 0)


def partial_sums(jobs, sizes, columns, cost, place, counts, near_rows, near_weights, lists, table, after):
    ny, nx, cap = sizes
    vmem = pl.BlockSpec(memory_space=pltpu.VMEM)
    smem = pl.BlockSpec(memory_space=pltpu.SMEM)
    anywhere = pl.BlockSpec(memory_space=pl.ANY)
    return pl.pallas_call(
        functools.partial(partials_kernel, jobs, sizes),
        in_specs=[smem, smem, smem, smem, vmem, vmem, anywhere],
        out_specs=[vmem] * len(jobs),
        scratch_shapes=[
            pltpu.VMEM((CHUNK, 128), jnp.float32),
        ],
        out_shape=[
            jax.ShapeDtypeStruct((nx, columns, 128), jnp.float32) for _ in jobs
        ],
        compiler_params=pltpu.CompilerParams(vmem_limit_bytes=24 * 1024 * 1024),
        cost_estimate=pl.CostEstimate(
            flops=0, bytes_accessed=cost, transcendentals=0
        ),
    )(place, counts, near_rows, near_weights, lists, table, after)


def moved(value, axis, by):
    count = lax.axis_size(axis)
    return lax.ppermute(value, axis, [(i, (i + by) % count) for i in range(count)])


def ordered(value, earlier):
    probe = earlier.reshape(-1)[0]
    return jnp.where(probe != probe, probe, value)


def assemble_kernel(spots, *refs):
    sources, (out_ref, sems) = refs[:-2], refs[-2:]
    copies = [
        pltpu.make_async_copy(
            sources[source].at[pl.ds(begin, size)], out_ref.at[pl.ds(target, size)], sems.at[i]
        )
        for i, (source, begin, size, target) in enumerate(spots)
    ]
    for copy in copies:
        copy.start()
    for copy in copies:
        copy.wait()


def gathered(own, make_lists):
    rows, block = own.shape
    nz, nc = lax.axis_size("z"), lax.axis_size("c")
    onward = [(z * nc, (z + 1) % nz * nc) for z in range(nz)]
    onward += [(z * nc + 1, (z - 1) % nz * nc + 1) for z in range(nz)]
    swapped = lambda value: moved(value, "c", 1)
    mate = swapped(own)
    lists = make_lists(mate)
    arrays, spots = [own, mate], [(0, 0, rows, 0), (1, 0, rows, nz * rows)]
    pair = jnp.concatenate([own, mate], 0)
    for step in range(1, nz // 2 + 1):
        last = step == nz // 2
        if step == 2:
            pair = ordered(pair, lists[0, -2, :1])
        pair = lax.ppermute(pair[:rows] if last else pair, ("z", "c"), onward)
        arrays += [pair, swapped(pair)]
        place = len(arrays)
        spots.append((place - 2, 0, rows, step * rows))
        if last:
            spots.append((place - 1, 0, rows, (nz + step) * rows))
        else:
            spots.append((place - 2, rows, rows, (nz + step) * rows))
            spots.append((place - 1, 0, rows, (2 * nz - step) * rows))
            spots.append((place - 1, rows, rows, (nz - step) * rows))
    anywhere = pl.BlockSpec(memory_space=pl.ANY)
    table = pl.pallas_call(
        functools.partial(assemble_kernel, tuple(spots)),
        in_specs=[anywhere] * len(arrays),
        out_specs=pl.BlockSpec(memory_space=pltpu.VMEM),
        scratch_shapes=[pltpu.SemaphoreType.DMA((len(spots),))],
        out_shape=jax.ShapeDtypeStruct((nc * nz * rows, block), own.dtype),
        compiler_params=pltpu.CompilerParams(vmem_limit_bytes=16 * 1024 * 1024),
    )(*arrays)
    return table, lists


def shifted(shard, axis, by):
    devices = lax.axis_size(axis)
    pairs = [(i, i + by) for i in range(devices) if 0 <= i + by < devices]
    return lax.ppermute(shard, axis, pairs)


SUB = ("z", "x", "c")


def log_conductivity(model, block_owner_rank, source_slot, weights):
    ny, nz, nx, nc = (lax.axis_size(a) for a in ("y", "z", "x", "c"))
    quarter, block = model.shape[0], model.shape[2]
    columns, top = weights.shape[1:]
    here = jnp.stack([lax.axis_index("z"), lax.axis_index("c")]).astype(jnp.int32)
    classes = ny * nx
    cap = min(columns * top, nz * nc * 128) + CHUNK
    sizes = (nz, nx, nc, quarter, classes, cap)

    def make_lists(after):
        return build_lists(
            sizes, here, block_owner_rank[0].T, source_slot[0].T, weights[0].T, after
        )

    table, lists = gathered(model.reshape(quarter, block), make_lists)
    lists = lax.all_to_all(lists, ("y", "x"), split_axis=0, concat_axis=0, tiled=True)
    lane_rows, near = cap // 128, NEAR // 128
    near_rows = lists[:, :near].reshape(-1).astype(jnp.int32)
    near_factors = lists[:, lane_rows : lane_rows + near].reshape(-1)
    counts = lists[:, FIELDS * lane_rows : FIELDS * lane_rows + 2, 0].T.reshape(-1).astype(jnp.int32)
    place = jnp.stack([lax.axis_index(a) for a in ("y", "x", "c")]).astype(jnp.int32)

    def sums(after, cost, *offsets):
        return partial_sums(
            offsets, (ny, nx, cap), columns, cost, place, counts, near_rows, near_factors, lists, table, after
        )

    def sent(value, by, turn):
        pairs = []
        for i in range(ny * nx * nc):
            y, x, c = i // (nx * nc), i // nc % nx, i % nc
            to_y, to_x = ((y + by) % ny, x) if c == turn else (y, (x + by) % nx)
            pairs.append((i, (to_y * nx + to_x) * nc + c))
        return lax.ppermute(value, ("y", "x", "c"), pairs)

    mib = 1024 * 1024
    (far,) = sums(place, 10 * mib, 2)
    up, down = sums(far, 40 * mib, 1, 3)
    far = sent(far, 2, 0)
    (near,) = sums(far, 40 * mib, 0)
    got = [sent(up, 1, 0), sent(down, 3, 0)]
    joined = [near[d] + far[d] + got[0][d] + got[1][d] for d in range(nx)]
    return sum((sent(joined[d], d, 1) for d in (2, 1, 3)), joined[0]), near


def next_along(value, axis):
    length = value.shape[axis]
    place = lax.broadcasted_iota(jnp.int32, value.shape, axis)
    return jnp.where(place == length - 1, 0.0, pltpu.roll(value, length - 1, axis))


def last_along(value, axis, edge):
    place = lax.broadcasted_iota(jnp.int32, value.shape, axis)
    return jnp.where(place == 0, edge, pltpu.roll(value, 1, axis))


def ahead(value, axis):
    return next_along(value, axis) - value


def behind(value, axis):
    return value - last_along(value, axis, 0.0)


def mean_along(value, axis):
    return 0.5 * (value + last_along(value, axis, value))


def curl_kernel(rim_ref, field_ref, before_ref, after_ref, source_ref, earlier_ref, out_ref):
    planes = field_ref.shape[2]
    rim = rim_ref[0]
    for part in range(2):

        def edges(i):
            ref, at = (before_ref, 0) if i < 0 else (after_ref, 0) if i == planes else (field_ref, i)
            return [ref[part, comp, at] for comp in range(3)]

        now, held_y, held_z = edges(-1), None, None
        for i in range(-1, planes):
            later = edges(i + 1)
            ex, ey, ez = now
            hy = ahead(ex, 1) - (later[2] - ez)
            hz = (later[1] - ey) - ahead(ex, 0)
            if i < 0:
                hy, hz = hy * rim, hz * rim
            else:
                hx = ahead(ez, 0) - ahead(ey, 1)
                curl = (
                    behind(hz, 0) - behind(hy, 1),
                    behind(hx, 1) - (hz - held_z),
                    (hy - held_y) - behind(hx, 0),
                )
                for comp in range(3):
                    out_ref[part, comp, i] = curl[comp] - source_ref[part, comp, i]
            now, held_y, held_z = later, hy, hz


def curl_less_source(rim, field, before, after, source, earlier):
    vmem = pl.BlockSpec(memory_space=pltpu.VMEM)
    return pl.pallas_call(
        curl_kernel,
        in_specs=[pl.BlockSpec(memory_space=pltpu.SMEM)] + [vmem] * 4 + [pl.BlockSpec(memory_space=pl.ANY)],
        out_specs=vmem,
        out_shape=jax.ShapeDtypeStruct(field.shape, jnp.float32),
        compiler_params=pltpu.CompilerParams(vmem_limit_bytes=16 * 1024 * 1024),
        cost_estimate=pl.CostEstimate(flops=0, bytes_accessed=12 * 1024 * 1024, transcendentals=0),
    )(rim, field, before, after, source, earlier)


def residual_kernel(omega_ref, log_ref, prior_ref, rest_ref, field_ref, out_ref, held, sems):
    planes = field_ref.shape[2]
    omega = omega_ref[0]
    conduct = prior_ref[...]
    held_z, held_y = mean_along(conduct, 1), mean_along(conduct, 0)
    copies = []
    for i in range(planes):
        conduct = jnp.exp(log_ref[i])
        mean_z, mean_y = mean_along(conduct, 1), mean_along(conduct, 0)
        sigma = (mean_along(mean_z, 0), 0.5 * (mean_z + held_z), 0.5 * (mean_y + held_y))
        for comp in range(3):
            scaled = omega * sigma[comp]
            held[0, comp, i] = rest_ref[0, comp, i] - scaled * field_ref[1, comp, i]
            held[1, comp, i] = rest_ref[1, comp, i] + scaled * field_ref[0, comp, i]
        held_z, held_y = mean_z, mean_y
        copies.append(pltpu.make_async_copy(held.at[:, :, i], out_ref.at[:, :, i], sems.at[i]))
        copies[-1].start()
    for copy in copies:
        copy.wait()


def residual(omega, log_cond, prior, rest, field):
    vmem = pl.BlockSpec(memory_space=pltpu.VMEM)
    return pl.pallas_call(
        residual_kernel,
        in_specs=[pl.BlockSpec(memory_space=pltpu.SMEM)] + [vmem] * 4,
        out_specs=pl.BlockSpec(memory_space=pl.ANY),
        out_shape=jax.ShapeDtypeStruct(field.shape, jnp.float32),
        scratch_shapes=[
            pltpu.VMEM(field.shape, jnp.float32),
            pltpu.SemaphoreType.DMA((field.shape[2],)),
        ],
        compiler_params=pltpu.CompilerParams(vmem_limit_bytes=16 * 1024 * 1024),
    )(omega, log_cond, prior, rest, field)


def per_device(model, block_owner_rank, source_slot, weights, field, source, freq):
    efield = field[0]
    planes, cells_y = efield.shape[2:4]
    first_device = lax.axis_index(SUB) == 0

    halos = [shifted(efield[:, :, -1:], SUB, 1), shifted(efield[:, :, :1], SUB, -1)]
    log_cond, near = log_conductivity(model, block_owner_rank, source_slot, weights)
    log_cond = log_cond.reshape(planes, cells_y, -1)
    rim = jnp.where(first_device, 0.0, 1.0).astype(jnp.float32)[None]
    rest = curl_less_source(rim, efield, *halos, source[0], near)
    prior = shifted(jnp.exp(log_cond[-1]), SUB, 1)
    prior = jnp.where(first_device, jnp.exp(log_cond[0]), prior)
    return residual(freq, log_cond, prior, rest, efield)[None]


def solution(mesh):
    fine = Mesh(mesh.devices.reshape(4, 8, 4, 2), ("y",) + SUB)
    in_specs = (
        P("y", SUB, None),
        P("y", SUB, None),
        P("y", SUB, None),
        P("y", SUB, None),
        P("y", None, None, SUB, None, None),
        P("y", None, None, SUB, None, None),
        P("y"),
    )
    out_specs = P("y", None, None, SUB, None, None)
    return jax.shard_map(
        per_device, mesh=fine, in_specs=in_specs, out_specs=out_specs, check_vma=False
    )
```

```python
import functools

import jax
import jax.numpy as jnp
from jax import lax
from jax.experimental import pallas as pl
from jax.experimental.pallas import tpu as pltpu
from jax.sharding import Mesh, PartitionSpec as P

CHUNK = 256
FIELDS = 3
STEP = 16
NEAR = 512


def shift_of(count):
    return (count - 1).bit_length()


def lists_kernel(sizes, here_ref, owner_far, slot_far, weight_far, after_ref, out_ref, values, *rest):
    nz, nx, nc, quarter, classes, cap = sizes
    top, columns = owner_far.shape
    owner_ref, slot_ref, weight_ref, sems = rest
    copies = [
        pltpu.make_async_copy(far, near, sems.at[i])
        for i, (far, near) in enumerate(
            ((owner_far, owner_ref), (slot_far, slot_ref), (weight_far, weight_ref))
        )
    ]
    for copy in copies:
        copy.start()
    for copy in copies:
        copy.wait()
    owner, slot, weight = owner_ref[...], slot_ref[...], weight_ref[...]
    bits_c, bits_x, bits_q = shift_of(nc), shift_of(nx), shift_of(quarter)
    kind = (slot >> bits_q) * nx + ((owner >> bits_c) & (nx - 1))
    layer = (((owner >> (bits_c + bits_x)) - here_ref[0]) * (2 * here_ref[1] - 1)) & (nz - 1)
    core = (owner - here_ref[1]) & (nc - 1)
    row = (core * nz + layer) * quarter + (slot & (quarter - 1))
    column = lax.broadcasted_iota(jnp.int32, (top, columns), 1)
    as_float = lambda value: value.astype(jnp.float32)
    rounded = lambda value: value.astype(jnp.bfloat16).astype(jnp.float32)
    high = rounded(weight)
    middle = rounded(weight - high)
    parts = [
        as_float(row >> 7),
        as_float(row & 127),
        as_float(column >> 8),
        as_float(column & 255),
        high,
        middle,
        weight - high - middle,
        jnp.zeros((top, columns), jnp.float32),
    ]
    iota_kind = lax.broadcasted_iota(jnp.int32, (classes, columns), 0)
    marks = []
    for k in range(top):
        mark = iota_kind == kind[k : k + 1, :]
        marks.append(jnp.where(mark, 1.0, 0.0))
        stacked = [jnp.where(mark, part[k : k + 1, :], 0.0) for part in parts]
        values[k] = jnp.concatenate(stacked, 0).astype(jnp.bfloat16)
    marks = jnp.concatenate(marks, 0)
    marks_low = marks.astype(jnp.bfloat16)
    rows = top * classes
    half = columns // 2
    column_i = lax.broadcasted_iota(jnp.int32, (columns, columns), 0)
    column_j = lax.broadcasted_iota(jnp.int32, (columns, columns), 1)
    before = (column_i < column_j) & ((column_i >= half) == (column_j >= half))
    prefix = jnp.dot(
        marks_low,
        jnp.where(before, 1.0, 0.0).astype(jnp.bfloat16),
        preferred_element_type=jnp.float32,
    )
    row_i = lax.broadcasted_iota(jnp.int32, (rows, rows), 0)
    row_j = lax.broadcasted_iota(jnp.int32, (rows, rows), 1)
    earlier = (row_j < row_i) & ((row_i & (classes - 1)) == (row_j & (classes - 1)))
    above = jnp.dot(
        jnp.where(earlier, 1.0, 0.0).astype(jnp.bfloat16),
        marks_low,
        preferred_element_type=jnp.float32,
    )
    over = lambda value: jnp.sum(value, axis=1, keepdims=True)

    def per_kind(value):
        sums = over(value)
        total = sums[:classes]
        for k in range(1, top):
            total = total + sums[k * classes : (k + 1) * classes]
        return total

    count_a, count_b = per_kind(marks[:, :half]), per_kind(marks[:, half:])
    begin_b = ((count_a.astype(jnp.int32) + 127) >> 7) << 7
    most = jnp.max(begin_b + count_b.astype(jnp.int32))
    begin_rows = jnp.concatenate([begin_b.astype(jnp.float32)] * top, 0)
    base_a, base_b = over(above[:, :half]), over(above[:, half:]) + begin_rows
    lanes = lax.broadcasted_iota(jnp.int32, (rows, columns), 1)
    placed = marks * (prefix + jnp.where(lanes < half, base_a, base_b))
    ranks = [
        jnp.sum(placed[k * classes : (k + 1) * classes], axis=0, keepdims=True).astype(jnp.int32)
        for k in range(top)
    ]
    lane_rows = cap // 128
    for f, total in enumerate((count_a, count_b)):
        spread = jnp.broadcast_to(total, (classes, 128))
        for c in range(classes):
            at = FIELDS * lane_rows + f
            out_ref[c, at : at + 1, :] = spread[c : c + 1, :]
    iota_rank = lax.broadcasted_iota(jnp.int32, (CHUNK, columns), 0)

    def one_chunk(j, carry):
        found = jnp.zeros((CHUNK, len(parts) * classes), jnp.float32)
        for k in range(top):
            hot = jnp.where(iota_rank == ranks[k] - j * CHUNK, 1.0, 0.0).astype(jnp.bfloat16)
            found = found + lax.dot_general(
                hot, values[k], (((1,), (1,)), ((), ())), preferred_element_type=jnp.float32
            )
        turned = found.T
        part = lambda p: turned[p * classes : (p + 1) * classes]
        fields = [
            part(0) * 128.0 + part(1),
            part(4) + part(5) + part(6),
            part(2) * 256.0 + part(3),
        ]
        for f in range(FIELDS):
            for h in range(CHUNK // 128):
                at = f * lane_rows + j * (CHUNK // 128) + h
                for c in range(classes):
                    out_ref[c, pl.ds(at, 1), :] = fields[f][c : c + 1, h * 128 : (h + 1) * 128]
        return carry

    lax.fori_loop(0, (most + CHUNK - 1) // CHUNK, one_chunk, 0)


def build_lists(sizes, here, owner, slot, weight, after):
    nz, nx, nc, quarter, classes, cap = sizes
    top, columns = owner.shape
    lane_rows = cap // 128
    return pl.pallas_call(
        functools.partial(lists_kernel, sizes),
        out_shape=jax.ShapeDtypeStruct((classes, -(-(FIELDS * lane_rows + 2) // 8) * 8, 128), jnp.float32),
        in_specs=[pl.BlockSpec(memory_space=pltpu.SMEM)] + [pl.BlockSpec(memory_space=pl.ANY)] * 4,
        out_specs=pl.BlockSpec(memory_space=pltpu.VMEM),
        scratch_shapes=[
            pltpu.VMEM((top, 8 * classes, columns), jnp.bfloat16),
            pltpu.VMEM((top, columns), jnp.int32),
            pltpu.VMEM((top, columns), jnp.int32),
            pltpu.VMEM((top, columns), jnp.float32),
            pltpu.SemaphoreType.DMA((3,)),
        ],
        cost_estimate=pl.CostEstimate(flops=0, bytes_accessed=12 * 1024 * 1024, transcendentals=0),
        compiler_params=pltpu.CompilerParams(vmem_limit_bytes=24 * 1024 * 1024),
    )(here, owner, slot, weight, after)


def partials_kernel(
    jobs, sizes, place_ref, count_ref, row_ref, weight_ref, list_ref, table_ref, *rest
):
    ny, nx, cap = sizes
    outs, picked = rest[-1 - len(jobs) : -1], rest[-1]
    columns = outs[0].shape[1] // 2
    lane_rows = cap // 128
    iota = lax.broadcasted_iota(jnp.int32, (columns, 128), 0)
    lanes = lax.broadcasted_iota(jnp.int32, (1, 128), 1)
    picked[...] = jnp.zeros_like(picked)

    def gather(slot, at, begin, count, j):
        first = begin + j * CHUNK
        left = jnp.minimum(count - j * CHUNK, CHUNK)
        near = first + CHUNK <= NEAR

        @pl.when(near)
        def _():
            start = at * NEAR + first

            def some(i, carry):
                base = pl.multiple_of(i * STEP, STEP)
                for u in range(STEP):
                    picked[slot, pl.ds(base + u, 1), :] = (
                        table_ref[pl.ds(row_ref[start + base + u], 1), :] * weight_ref[start + base + u]
                    )
                return carry

            lax.fori_loop(0, (left + STEP - 1) // STEP, some, 0)

        @pl.when(jnp.logical_not(near))
        def _():
            def single(u, carry):
                line = lax.shift_right_logical(first + u, 7)
                here = lanes == jnp.bitwise_and(first + u, 127)
                pick = lambda f: jnp.sum(
                    jnp.where(here, list_ref[at, pl.ds(f * lane_rows + line, 1), :], 0.0)
                )
                row = pick(0).astype(jnp.int32)
                picked[slot, pl.ds(u, 1), :] = table_ref[pl.ds(row, 1), :] * pick(1)
                return carry

            lax.fori_loop(0, left, single, 0)

    def combine(slot, half, at, begin, count, j):
        first = begin + j * CHUNK
        left = count - j * CHUNK
        rows = picked[slot]
        high = rows.astype(jnp.bfloat16)
        low = (rows - high.astype(jnp.float32)).astype(jnp.bfloat16)
        hot = []
        for h in range(CHUNK // 128):
            line = 2 * lane_rows + lax.shift_right_logical(first, 7) + h
            place = list_ref[at, pl.ds(line, 1), :].astype(jnp.int32) - half * columns
            place = jnp.where(lanes < left - h * 128, place, -1)
            hot.append(jnp.where(iota == place, 1.0, 0.0).astype(jnp.bfloat16))
        summed = jnp.dot(
            jnp.concatenate(hot, 1), jnp.concatenate([high, low], 1), preferred_element_type=jnp.float32
        )
        return summed[:, :128] + summed[:, 128:]

    tasks = []
    for (offset, begin_t), out_ref in zip(jobs, outs):
        for step in range(out_ref.shape[0]):
            t, swap = begin_t + step, place_ref[2]
            y = (place_ref[0] + jnp.where(swap == 0, offset, t)) % ny
            x = (place_ref[1] + jnp.where(swap == 0, t, offset)) % nx
            at = y * nx + x
            count_a = count_ref[at]
            begin_b = lax.shift_left(lax.shift_right_logical(count_a + 127, 7), 7)
            tasks.append((out_ref, step, 0, at, 0, count_a))
            tasks.append((out_ref, step, 1, at, begin_b, count_ref[ny * nx + at]))
    for slot, (_, _, _, at, begin, count) in enumerate(tasks):
        gather(slot, at, begin, count, 0)
    for slot, (out_ref, step, half, at, begin, count) in enumerate(tasks):
        out_ref[step, half * columns : (half + 1) * columns, :] = combine(slot, half, at, begin, count, 0)
    for out_ref, step, half, at, begin, count in tasks:

        def more(j, carry):
            gather(0, at, begin, count, j)
            out_ref[step, half * columns : (half + 1) * columns, :] += combine(0, half, at, begin, count, j)
            return carry

        lax.fori_loop(1, (count + CHUNK - 1) // CHUNK, more, 0)


def partial_sums(jobs, sizes, columns, cost, place, counts, near_rows, near_weights, lists, table, after):
    ny, nx, cap = sizes
    vmem = pl.BlockSpec(memory_space=pltpu.VMEM)
    smem = pl.BlockSpec(memory_space=pltpu.SMEM)
    anywhere = pl.BlockSpec(memory_space=pl.ANY)
    return pl.pallas_call(
        functools.partial(partials_kernel, [job[:2] for job in jobs], sizes),
        in_specs=[smem, smem, smem, smem, vmem, vmem] + [anywhere] * len(after),
        out_specs=[vmem] * len(jobs),
        scratch_shapes=[
            pltpu.VMEM((2 * sum(job[2] for job in jobs), CHUNK, 128), jnp.float32),
        ],
        out_shape=[
            jax.ShapeDtypeStruct((job[2], columns, 128), jnp.float32) for job in jobs
        ],
        compiler_params=pltpu.CompilerParams(vmem_limit_bytes=24 * 1024 * 1024),
        cost_estimate=pl.CostEstimate(
            flops=0, bytes_accessed=cost, transcendentals=0
        ),
    )(place, counts, near_rows, near_weights, lists, table, *after)


def moved(value, axis, by):
    count = lax.axis_size(axis)
    return lax.ppermute(value, axis, [(i, (i + by) % count) for i in range(count)])


def ordered(value, earlier):
    probe = earlier.reshape(-1)[0]
    return jnp.where(probe != probe, probe, value)


def assemble_kernel(spots, *refs):
    sources, (out_ref, sems) = refs[:-2], refs[-2:]
    copies = [
        pltpu.make_async_copy(
            sources[source].at[pl.ds(begin, size)], out_ref.at[pl.ds(target, size)], sems.at[i]
        )
        for i, (source, begin, size, target) in enumerate(spots)
    ]
    for copy in copies:
        copy.start()
    for copy in copies:
        copy.wait()


def gathered(own, make_lists):
    rows, block = own.shape
    nz, nc = lax.axis_size("z"), lax.axis_size("c")
    onward = [(z * nc, (z + 1) % nz * nc) for z in range(nz)]
    onward += [(z * nc + 1, (z - 1) % nz * nc + 1) for z in range(nz)]
    swapped = lambda value: moved(value, "c", 1)
    mate = swapped(own)
    lists = make_lists(mate)
    arrays, spots = [], []

    def take(array, spot):
        spots.append((len(arrays), 0, array.shape[0], spot * rows))
        arrays.append(array)

    take(own, 0)
    take(mate, nz)
    pair = [own, mate]
    for step in range(1, nz // 2 + 1):
        if step == 2:
            pair[0] = ordered(pair[0], lists[0, -2, :1])
        if step == nz // 2:
            pair = pair[:1]
        pair = [lax.ppermute(one, ("z", "c"), onward) for one in pair]
        for core, one in enumerate(pair):
            take(one, core * nz + step)
            take(swapped(one), (1 - core) * nz + nz - step)
    anywhere = pl.BlockSpec(memory_space=pl.ANY)
    table = pl.pallas_call(
        functools.partial(assemble_kernel, tuple(spots)),
        in_specs=[anywhere] * len(arrays),
        out_specs=pl.BlockSpec(memory_space=pltpu.VMEM),
        scratch_shapes=[pltpu.SemaphoreType.DMA((len(spots),))],
        out_shape=jax.ShapeDtypeStruct((nc * nz * rows, block), own.dtype),
        compiler_params=pltpu.CompilerParams(vmem_limit_bytes=16 * 1024 * 1024),
    )(*arrays)
    return table, lists


def shifted(shard, axis, by):
    devices = lax.axis_size(axis)
    pairs = [(i, i + by) for i in range(devices) if 0 <= i + by < devices]
    return lax.ppermute(shard, axis, pairs)


SUB = ("z", "x", "c")


def log_conductivity(model, block_owner_rank, source_slot, weights):
    ny, nz, nx, nc = (lax.axis_size(a) for a in ("y", "z", "x", "c"))
    quarter, block = model.shape[0], model.shape[2]
    columns, top = weights.shape[1:]
    here = jnp.stack([lax.axis_index("z"), lax.axis_index("c")]).astype(jnp.int32)
    classes = ny * nx
    cap = min(columns * top, nz * nc * 128) + CHUNK
    sizes = (nz, nx, nc, quarter, classes, cap)

    def make_lists(after):
        return build_lists(
            sizes, here, block_owner_rank[0].T, source_slot[0].T, weights[0].T, after
        )

    table, lists = gathered(model.reshape(quarter, block), make_lists)
    lists = lax.all_to_all(lists, ("y", "x"), split_axis=0, concat_axis=0, tiled=True)
    lane_rows, near = cap // 128, NEAR // 128
    near_rows = lists[:, :near].reshape(-1).astype(jnp.int32)
    near_factors = lists[:, lane_rows : lane_rows + near].reshape(-1)
    counts = lists[:, FIELDS * lane_rows : FIELDS * lane_rows + 2, 0].T.reshape(-1).astype(jnp.int32)
    place = jnp.stack([lax.axis_index(a) for a in ("y", "x", "c")]).astype(jnp.int32)

    def sums(after, cost, *offsets):
        return partial_sums(
            offsets, (ny, nx, cap), columns, cost, place, counts, near_rows, near_factors, lists, table, after
        )

    def sent(value, by, turn):
        pairs = []
        for i in range(ny * nx * nc):
            y, x, c = i // (nx * nc), i // nc % nx, i % nc
            to_y, to_x = ((y + by) % ny, x) if c == turn else (y, (x + by) % nx)
            pairs.append((i, (to_y * nx + to_x) * nc + c))
        return lax.ppermute(value, ("y", "x", "c"), pairs)

    mib = 1024 * 1024
    (far,) = sums((), 10 * mib, (2, 0, nx))
    up, down = sums((far,), 40 * mib, (1, 0, nx), (3, 0, nx))
    far = sent(far, 2, 0)
    (near,) = sums((far,), 40 * mib, (0, 0, nx))
    got = [far, sent(up, 1, 0), sent(down, 3, 0)]
    joined = [near[d] + got[0][d] + got[1][d] + got[2][d] for d in range(nx)]
    return sum((sent(joined[d], d, 1) for d in (2, 1, 3)), joined[0]), near


def next_along(value, axis):
    length = value.shape[axis]
    place = lax.broadcasted_iota(jnp.int32, value.shape, axis)
    return jnp.where(place == length - 1, 0.0, pltpu.roll(value, length - 1, axis))


def last_along(value, axis, edge):
    place = lax.broadcasted_iota(jnp.int32, value.shape, axis)
    return jnp.where(place == 0, edge, pltpu.roll(value, 1, axis))


def ahead(value, axis):
    return next_along(value, axis) - value


def behind(value, axis):
    return value - last_along(value, axis, 0.0)


def mean_along(value, axis):
    return 0.5 * (value + last_along(value, axis, value))


def curl_kernel(rim_ref, field_ref, before_ref, after_ref, source_ref, earlier_ref, out_ref):
    planes = field_ref.shape[2]
    rim = rim_ref[0]
    for part in range(2):

        def edges(i):
            ref, at = (before_ref, 0) if i < 0 else (after_ref, 0) if i == planes else (field_ref, i)
            return [ref[part, comp, at] for comp in range(3)]

        now, held_y, held_z = edges(-1), None, None
        for i in range(-1, planes):
            later = edges(i + 1)
            ex, ey, ez = now
            hy = ahead(ex, 1) - (later[2] - ez)
            hz = (later[1] - ey) - ahead(ex, 0)
            if i < 0:
                hy, hz = hy * rim, hz * rim
            else:
                hx = ahead(ez, 0) - ahead(ey, 1)
                curl = (
                    behind(hz, 0) - behind(hy, 1),
                    behind(hx, 1) - (hz - held_z),
                    (hy - held_y) - behind(hx, 0),
                )
                for comp in range(3):
                    out_ref[part, comp, i] = curl[comp] - source_ref[part, comp, i]
            now, held_y, held_z = later, hy, hz


def curl_less_source(rim, field, before, after, source, earlier):
    vmem = pl.BlockSpec(memory_space=pltpu.VMEM)
    return pl.pallas_call(
        curl_kernel,
        in_specs=[pl.BlockSpec(memory_space=pltpu.SMEM)] + [vmem] * 4 + [pl.BlockSpec(memory_space=pl.ANY)],
        out_specs=vmem,
        out_shape=jax.ShapeDtypeStruct(field.shape, jnp.float32),
        compiler_params=pltpu.CompilerParams(vmem_limit_bytes=16 * 1024 * 1024),
        cost_estimate=pl.CostEstimate(flops=0, bytes_accessed=12 * 1024 * 1024, transcendentals=0),
    )(rim, field, before, after, source, earlier)


def residual_kernel(omega_ref, log_ref, prior_ref, rest_ref, field_ref, out_ref, held, sems):
    planes = field_ref.shape[2]
    omega = omega_ref[0]
    conduct = prior_ref[...]
    held_z, held_y = mean_along(conduct, 1), mean_along(conduct, 0)
    copies = []
    for i in range(planes):
        conduct = jnp.exp(log_ref[i])
        mean_z, mean_y = mean_along(conduct, 1), mean_along(conduct, 0)
        sigma = (mean_along(mean_z, 0), 0.5 * (mean_z + held_z), 0.5 * (mean_y + held_y))
        for comp in range(3):
            scaled = omega * sigma[comp]
            held[0, comp, i] = rest_ref[0, comp, i] - scaled * field_ref[1, comp, i]
            held[1, comp, i] = rest_ref[1, comp, i] + scaled * field_ref[0, comp, i]
        held_z, held_y = mean_z, mean_y
        copies.append(pltpu.make_async_copy(held.at[:, :, i], out_ref.at[:, :, i], sems.at[i]))
        copies[-1].start()
    for copy in copies:
        copy.wait()


def residual(omega, log_cond, prior, rest, field):
    vmem = pl.BlockSpec(memory_space=pltpu.VMEM)
    return pl.pallas_call(
        residual_kernel,
        in_specs=[pl.BlockSpec(memory_space=pltpu.SMEM)] + [vmem] * 4,
        out_specs=pl.BlockSpec(memory_space=pl.ANY),
        out_shape=jax.ShapeDtypeStruct(field.shape, jnp.float32),
        scratch_shapes=[
            pltpu.VMEM(field.shape, jnp.float32),
            pltpu.SemaphoreType.DMA((field.shape[2],)),
        ],
        compiler_params=pltpu.CompilerParams(vmem_limit_bytes=16 * 1024 * 1024),
    )(omega, log_cond, prior, rest, field)


def per_device(model, block_owner_rank, source_slot, weights, field, source, freq):
    efield = field[0]
    planes, cells_y = efield.shape[2:4]
    first_device = lax.axis_index(SUB) == 0

    halos = [shifted(efield[:, :, -1:], SUB, 1), shifted(efield[:, :, :1], SUB, -1)]
    log_cond, near = log_conductivity(model, block_owner_rank, source_slot, weights)
    log_cond = log_cond.reshape(planes, cells_y, -1)
    rim = jnp.where(first_device, 0.0, 1.0).astype(jnp.float32)[None]
    rest = curl_less_source(rim, efield, *halos, source[0], near)
    prior = shifted(jnp.exp(log_cond[-1]), SUB, 1)
    prior = jnp.where(first_device, jnp.exp(log_cond[0]), prior)
    return residual(freq, log_cond, prior, rest, efield)[None]


def solution(mesh):
    fine = Mesh(mesh.devices.reshape(4, 8, 4, 2), ("y",) + SUB)
    in_specs = (
        P("y", SUB, None),
        P("y", SUB, None),
        P("y", SUB, None),
        P("y", SUB, None),
        P("y", None, None, SUB, None, None),
        P("y", None, None, SUB, None, None),
        P("y"),
    )
    out_specs = P("y", None, None, SUB, None, None)
    return jax.shard_map(
        per_device, mesh=fine, in_specs=in_specs, out_specs=out_specs, check_vma=False
    )
```

```python
import functools

import jax
import jax.numpy as jnp
from jax import lax
from jax.experimental import pallas as pl
from jax.experimental.pallas import tpu as pltpu
from jax.sharding import Mesh, PartitionSpec as P

CHUNK = 256
FIELDS = 3
STEP = 16
NEAR = 512


def shift_of(count):
    return (count - 1).bit_length()


def lists_kernel(sizes, here_ref, owner_far, slot_far, weight_far, after_ref, out_ref, values, *rest):
    nz, nx, nc, quarter, classes, cap = sizes
    top, columns = owner_far.shape
    owner_ref, slot_ref, weight_ref, sems = rest
    copies = [
        pltpu.make_async_copy(far, near, sems.at[i])
        for i, (far, near) in enumerate(
            ((owner_far, owner_ref), (slot_far, slot_ref), (weight_far, weight_ref))
        )
    ]
    for copy in copies:
        copy.start()
    for copy in copies:
        copy.wait()
    owner, slot, weight = owner_ref[...], slot_ref[...], weight_ref[...]
    bits_c, bits_x, bits_q = shift_of(nc), shift_of(nx), shift_of(quarter)
    kind = (slot >> bits_q) * nx + ((owner >> bits_c) & (nx - 1))
    layer = (((owner >> (bits_c + bits_x)) - here_ref[0]) * (2 * here_ref[1] - 1)) & (nz - 1)
    core = (owner - here_ref[1]) & (nc - 1)
    row = (core * nz + layer) * quarter + (slot & (quarter - 1))
    column = lax.broadcasted_iota(jnp.int32, (top, columns), 1)
    as_float = lambda value: value.astype(jnp.float32)
    rounded = lambda value: value.astype(jnp.bfloat16).astype(jnp.float32)
    high = rounded(weight)
    middle = rounded(weight - high)
    parts = [
        as_float(row >> 7),
        as_float(row & 127),
        as_float(column >> 8),
        as_float(column & 255),
        high,
        middle,
        weight - high - middle,
        jnp.zeros((top, columns), jnp.float32),
    ]
    iota_kind = lax.broadcasted_iota(jnp.int32, (classes, columns), 0)
    marks = []
    for k in range(top):
        mark = iota_kind == kind[k : k + 1, :]
        marks.append(jnp.where(mark, 1.0, 0.0))
        stacked = [jnp.where(mark, part[k : k + 1, :], 0.0) for part in parts]
        values[k] = jnp.concatenate(stacked, 0).astype(jnp.bfloat16)
    marks = jnp.concatenate(marks, 0)
    marks_low = marks.astype(jnp.bfloat16)
    rows = top * classes
    half = columns // 2
    column_i = lax.broadcasted_iota(jnp.int32, (columns, columns), 0)
    column_j = lax.broadcasted_iota(jnp.int32, (columns, columns), 1)
    before = (column_i < column_j) & ((column_i >= half) == (column_j >= half))
    prefix = jnp.dot(
        marks_low,
        jnp.where(before, 1.0, 0.0).astype(jnp.bfloat16),
        preferred_element_type=jnp.float32,
    )
    row_i = lax.broadcasted_iota(jnp.int32, (rows, rows), 0)
    row_j = lax.broadcasted_iota(jnp.int32, (rows, rows), 1)
    earlier = (row_j < row_i) & ((row_i & (classes - 1)) == (row_j & (classes - 1)))
    above = jnp.dot(
        jnp.where(earlier, 1.0, 0.0).astype(jnp.bfloat16),
        marks_low,
        preferred_element_type=jnp.float32,
    )
    over = lambda value: jnp.sum(value, axis=1, keepdims=True)

    def per_kind(value):
        sums = over(value)
        total = sums[:classes]
        for k in range(1, top):
            total = total + sums[k * classes : (k + 1) * classes]
        return total

    count_a, count_b = per_kind(marks[:, :half]), per_kind(marks[:, half:])
    begin_b = ((count_a.astype(jnp.int32) + 127) >> 7) << 7
    most = jnp.max(begin_b + count_b.astype(jnp.int32))
    begin_rows = jnp.concatenate([begin_b.astype(jnp.float32)] * top, 0)
    base_a, base_b = over(above[:, :half]), over(above[:, half:]) + begin_rows
    lanes = lax.broadcasted_iota(jnp.int32, (rows, columns), 1)
    placed = marks * (prefix + jnp.where(lanes < half, base_a, base_b))
    ranks = [
        jnp.sum(placed[k * classes : (k + 1) * classes], axis=0, keepdims=True).astype(jnp.int32)
        for k in range(top)
    ]
    lane_rows = cap // 128
    for f, total in enumerate((count_a, count_b)):
        spread = jnp.broadcast_to(total, (classes, 128))
        for c in range(classes):
            at = FIELDS * lane_rows + f
            out_ref[c, at : at + 1, :] = spread[c : c + 1, :]
    iota_rank = lax.broadcasted_iota(jnp.int32, (CHUNK, columns), 0)

    def one_chunk(j, carry):
        found = jnp.zeros((CHUNK, len(parts) * classes), jnp.float32)
        for k in range(top):
            hot = jnp.where(iota_rank == ranks[k] - j * CHUNK, 1.0, 0.0).astype(jnp.bfloat16)
            found = found + lax.dot_general(
                hot, values[k], (((1,), (1,)), ((), ())), preferred_element_type=jnp.float32
            )
        turned = found.T
        part = lambda p: turned[p * classes : (p + 1) * classes]
        fields = [
            part(0) * 128.0 + part(1),
            part(4) + part(5) + part(6),
            part(2) * 256.0 + part(3),
        ]
        for f in range(FIELDS):
            for h in range(CHUNK // 128):
                at = f * lane_rows + j * (CHUNK // 128) + h
                for c in range(classes):
                    out_ref[c, pl.ds(at, 1), :] = fields[f][c : c + 1, h * 128 : (h + 1) * 128]
        return carry

    lax.fori_loop(0, (most + CHUNK - 1) // CHUNK, one_chunk, 0)


def build_lists(sizes, here, owner, slot, weight, after):
    nz, nx, nc, quarter, classes, cap = sizes
    top, columns = owner.shape
    lane_rows = cap // 128
    return pl.pallas_call(
        functools.partial(lists_kernel, sizes),
        out_shape=jax.ShapeDtypeStruct((classes, -(-(FIELDS * lane_rows + 2) // 8) * 8, 128), jnp.float32),
        in_specs=[pl.BlockSpec(memory_space=pltpu.SMEM)] + [pl.BlockSpec(memory_space=pl.ANY)] * 4,
        out_specs=pl.BlockSpec(memory_space=pltpu.VMEM),
        scratch_shapes=[
            pltpu.VMEM((top, 8 * classes, columns), jnp.bfloat16),
            pltpu.VMEM((top, columns), jnp.int32),
            pltpu.VMEM((top, columns), jnp.int32),
            pltpu.VMEM((top, columns), jnp.float32),
            pltpu.SemaphoreType.DMA((3,)),
        ],
        cost_estimate=pl.CostEstimate(flops=0, bytes_accessed=12 * 1024 * 1024, transcendentals=0),
        compiler_params=pltpu.CompilerParams(vmem_limit_bytes=24 * 1024 * 1024),
    )(here, owner, slot, weight, after)


def partials_kernel(
    jobs, sizes, place_ref, count_ref, row_ref, weight_ref, list_ref, table_ref, *rest
):
    ny, nx, cap = sizes
    outs, picked = rest[-1 - len(jobs) : -1], rest[-1]
    columns = outs[0].shape[1] // 2
    lane_rows = cap // 128
    iota = lax.broadcasted_iota(jnp.int32, (columns, 128), 0)
    lanes = lax.broadcasted_iota(jnp.int32, (1, 128), 1)
    picked[...] = jnp.zeros_like(picked)

    def gather(slot, at, begin, count, j):
        first = begin + j * CHUNK
        left = jnp.minimum(count - j * CHUNK, CHUNK)
        near = first + CHUNK <= NEAR

        @pl.when(near)
        def _():
            start = at * NEAR + first

            def some(i, carry):
                base = pl.multiple_of(i * STEP, STEP)
                for u in range(STEP):
                    picked[slot, pl.ds(base + u, 1), :] = (
                        table_ref[pl.ds(row_ref[start + base + u], 1), :] * weight_ref[start + base + u]
                    )
                return carry

            lax.fori_loop(0, (left + STEP - 1) // STEP, some, 0)

        @pl.when(jnp.logical_not(near))
        def _():
            def single(u, carry):
                line = lax.shift_right_logical(first + u, 7)
                here = lanes == jnp.bitwise_and(first + u, 127)
                pick = lambda f: jnp.sum(
                    jnp.where(here, list_ref[at, pl.ds(f * lane_rows + line, 1), :], 0.0)
                )
                row = pick(0).astype(jnp.int32)
                picked[slot, pl.ds(u, 1), :] = table_ref[pl.ds(row, 1), :] * pick(1)
                return carry

            lax.fori_loop(0, left, single, 0)

    def combine(slot, half, at, begin, count, j):
        first = begin + j * CHUNK
        left = count - j * CHUNK
        rows = picked[slot]
        high = rows.astype(jnp.bfloat16)
        low = (rows - high.astype(jnp.float32)).astype(jnp.bfloat16)
        hot = []
        for h in range(CHUNK // 128):
            line = 2 * lane_rows + lax.shift_right_logical(first, 7) + h
            place = list_ref[at, pl.ds(line, 1), :].astype(jnp.int32) - half * columns
            place = jnp.where(lanes < left - h * 128, place, -1)
            hot.append(jnp.where(iota == place, 1.0, 0.0).astype(jnp.bfloat16))
        summed = jnp.dot(
            jnp.concatenate(hot, 1), jnp.concatenate([high, low], 1), preferred_element_type=jnp.float32
        )
        return summed[:, :128] + summed[:, 128:]

    tasks = []
    for (offset, begin_t), out_ref in zip(jobs, outs):
        for step in range(out_ref.shape[0]):
            t, swap = begin_t + step, place_ref[2]
            y = (place_ref[0] + jnp.where(swap == 0, offset, t)) % ny
            x = (place_ref[1] + jnp.where(swap == 0, t, offset)) % nx
            at = y * nx + x
            count_a = count_ref[at]
            begin_b = lax.shift_left(lax.shift_right_logical(count_a + 127, 7), 7)
            tasks.append((out_ref, step, 0, at, 0, count_a))
            tasks.append((out_ref, step, 1, at, begin_b, count_ref[ny * nx + at]))
    for slot, (_, _, _, at, begin, count) in enumerate(tasks):
        gather(slot, at, begin, count, 0)
    for slot, (out_ref, step, half, at, begin, count) in enumerate(tasks):
        out_ref[step, half * columns : (half + 1) * columns, :] = combine(slot, half, at, begin, count, 0)
    for out_ref, step, half, at, begin, count in tasks:

        def more(j, carry):
            gather(0, at, begin, count, j)
            out_ref[step, half * columns : (half + 1) * columns, :] += combine(0, half, at, begin, count, j)
            return carry

        lax.fori_loop(1, (count + CHUNK - 1) // CHUNK, more, 0)


def partial_sums(jobs, sizes, columns, cost, place, counts, near_rows, near_weights, lists, table, after):
    ny, nx, cap = sizes
    vmem = pl.BlockSpec(memory_space=pltpu.VMEM)
    smem = pl.BlockSpec(memory_space=pltpu.SMEM)
    anywhere = pl.BlockSpec(memory_space=pl.ANY)
    return pl.pallas_call(
        functools.partial(partials_kernel, [job[:2] for job in jobs], sizes),
        in_specs=[smem, smem, smem, smem, vmem, vmem] + [anywhere] * len(after),
        out_specs=[vmem] * len(jobs),
        scratch_shapes=[
            pltpu.VMEM((2 * sum(job[2] for job in jobs), CHUNK, 128), jnp.float32),
        ],
        out_shape=[
            jax.ShapeDtypeStruct((job[2], columns, 128), jnp.float32) for job in jobs
        ],
        compiler_params=pltpu.CompilerParams(vmem_limit_bytes=24 * 1024 * 1024),
        cost_estimate=pl.CostEstimate(
            flops=0, bytes_accessed=cost, transcendentals=0
        ),
    )(place, counts, near_rows, near_weights, lists, table, *after)


def moved(value, axis, by):
    count = lax.axis_size(axis)
    return lax.ppermute(value, axis, [(i, (i + by) % count) for i in range(count)])


def ordered(value, *earlier):
    anywhere = pl.BlockSpec(memory_space=pl.ANY)
    return pl.pallas_call(
        lambda *refs: None,
        in_specs=[anywhere] * (1 + len(earlier)),
        out_specs=anywhere,
        out_shape=jax.ShapeDtypeStruct(value.shape, value.dtype),
        input_output_aliases={0: 0},
        compiler_params=pltpu.CompilerParams(vmem_limit_bytes=1024 * 1024),
    )(value, *earlier)


def assemble_kernel(spots, *refs):
    sources, (out_ref, sems) = refs[:-2], refs[-2:]
    copies = [
        pltpu.make_async_copy(
            sources[source].at[pl.ds(begin, size)], out_ref.at[pl.ds(target, size)], sems.at[i]
        )
        for i, (source, begin, size, target) in enumerate(spots)
    ]
    for copy in copies:
        copy.start()
    for copy in copies:
        copy.wait()


def gathered(own, make_lists):
    rows, block = own.shape
    nz, nc = lax.axis_size("z"), lax.axis_size("c")
    onward = [(z * nc, (z + 1) % nz * nc) for z in range(nz)]
    onward += [(z * nc + 1, (z - 1) % nz * nc + 1) for z in range(nz)]
    swapped = lambda value: moved(value, "c", 1)
    mate = swapped(own)
    lists = make_lists(mate)
    arrays, spots = [], []

    def take(array, spot):
        spots.append((len(arrays), 0, array.shape[0], spot * rows))
        arrays.append(array)

    take(own, 0)
    take(mate, nz)
    pair = [own, mate]
    for step in range(1, nz // 2 + 1):
        if step == nz // 2:
            pair = pair[:1]
        pair = [lax.ppermute(one, ("z", "c"), onward) for one in pair]
        if step == 1:
            pair[0] = ordered(pair[0], lists)
        elif step < nz // 2:
            pair[0] = ordered(pair[0], mates)
        mates = pair[-1]
        for core, one in enumerate(pair):
            take(one, core * nz + step)
            take(swapped(one), (1 - core) * nz + nz - step)
    anywhere = pl.BlockSpec(memory_space=pl.ANY)
    table = pl.pallas_call(
        functools.partial(assemble_kernel, tuple(spots)),
        in_specs=[anywhere] * len(arrays),
        out_specs=pl.BlockSpec(memory_space=pltpu.VMEM),
        scratch_shapes=[pltpu.SemaphoreType.DMA((len(spots),))],
        out_shape=jax.ShapeDtypeStruct((nc * nz * rows, block), own.dtype),
        compiler_params=pltpu.CompilerParams(vmem_limit_bytes=16 * 1024 * 1024),
    )(*arrays)
    return table, lists


def shifted(shard, axis, by):
    devices = lax.axis_size(axis)
    pairs = [(i, i + by) for i in range(devices) if 0 <= i + by < devices]
    return lax.ppermute(shard, axis, pairs)


SUB = ("z", "x", "c")


def log_conductivity(model, block_owner_rank, source_slot, weights):
    ny, nz, nx, nc = (lax.axis_size(a) for a in ("y", "z", "x", "c"))
    quarter, block = model.shape[0], model.shape[2]
    columns, top = weights.shape[1:]
    here = jnp.stack([lax.axis_index("z"), lax.axis_index("c")]).astype(jnp.int32)
    classes = ny * nx
    cap = min(columns * top, nz * nc * 128) + CHUNK
    sizes = (nz, nx, nc, quarter, classes, cap)

    def make_lists(after):
        return build_lists(
            sizes, here, block_owner_rank[0].T, source_slot[0].T, weights[0].T, after
        )

    table, lists = gathered(model.reshape(quarter, block), make_lists)
    lists = lax.all_to_all(lists, ("y", "x"), split_axis=0, concat_axis=0, tiled=True)
    lane_rows, near = cap // 128, NEAR // 128
    near_rows = lists[:, :near].reshape(-1).astype(jnp.int32)
    near_factors = lists[:, lane_rows : lane_rows + near].reshape(-1)
    counts = lists[:, FIELDS * lane_rows : FIELDS * lane_rows + 2, 0].T.reshape(-1).astype(jnp.int32)
    place = jnp.stack([lax.axis_index(a) for a in ("y", "x", "c")]).astype(jnp.int32)

    def sums(after, cost, *offsets):
        return partial_sums(
            offsets, (ny, nx, cap), columns, cost, place, counts, near_rows, near_factors, lists, table, after
        )

    def sent(value, by, turn):
        pairs = []
        for i in range(ny * nx * nc):
            y, x, c = i // (nx * nc), i // nc % nx, i % nc
            to_y, to_x = ((y + by) % ny, x) if c == turn else (y, (x + by) % nx)
            pairs.append((i, (to_y * nx + to_x) * nc + c))
        return lax.ppermute(value, ("y", "x", "c"), pairs)

    mib = 1024 * 1024
    (far,) = sums((), 10 * mib, (2, 0, nx))
    up, down = sums((far,), 40 * mib, (1, 0, nx), (3, 0, nx))
    far = sent(far, 2, 0)
    (near,) = sums((far,), 40 * mib, (0, 0, nx))
    got = [far, sent(up, 1, 0), sent(down, 3, 0)]
    joined = [near[d] + got[0][d] + got[1][d] + got[2][d] for d in range(nx)]
    return sum((sent(joined[d], d, 1) for d in (2, 1, 3)), joined[0]), near


def next_along(value, axis):
    length = value.shape[axis]
    place = lax.broadcasted_iota(jnp.int32, value.shape, axis)
    return jnp.where(place == length - 1, 0.0, pltpu.roll(value, length - 1, axis))


def last_along(value, axis, edge):
    place = lax.broadcasted_iota(jnp.int32, value.shape, axis)
    return jnp.where(place == 0, edge, pltpu.roll(value, 1, axis))


def ahead(value, axis):
    return next_along(value, axis) - value


def behind(value, axis):
    return value - last_along(value, axis, 0.0)


def mean_along(value, axis):
    return 0.5 * (value + last_along(value, axis, value))


def curl_kernel(rim_ref, field_ref, before_ref, after_ref, source_ref, earlier_ref, out_ref):
    planes = field_ref.shape[2]
    rim = rim_ref[0]
    for part in range(2):

        def edges(i):
            ref, at = (before_ref, 0) if i < 0 else (after_ref, 0) if i == planes else (field_ref, i)
            return [ref[part, comp, at] for comp in range(3)]

        now, held_y, held_z = edges(-1), None, None
        for i in range(-1, planes):
            later = edges(i + 1)
            ex, ey, ez = now
            hy = ahead(ex, 1) - (later[2] - ez)
            hz = (later[1] - ey) - ahead(ex, 0)
            if i < 0:
                hy, hz = hy * rim, hz * rim
            else:
                hx = ahead(ez, 0) - ahead(ey, 1)
                curl = (
                    behind(hz, 0) - behind(hy, 1),
                    behind(hx, 1) - (hz - held_z),
                    (hy - held_y) - behind(hx, 0),
                )
                for comp in range(3):
                    out_ref[part, comp, i] = curl[comp] - source_ref[part, comp, i]
            now, held_y, held_z = later, hy, hz


def curl_less_source(rim, field, before, after, source, earlier):
    vmem = pl.BlockSpec(memory_space=pltpu.VMEM)
    return pl.pallas_call(
        curl_kernel,
        in_specs=[pl.BlockSpec(memory_space=pltpu.SMEM)] + [vmem] * 4 + [pl.BlockSpec(memory_space=pl.ANY)],
        out_specs=vmem,
        out_shape=jax.ShapeDtypeStruct(field.shape, jnp.float32),
        compiler_params=pltpu.CompilerParams(vmem_limit_bytes=16 * 1024 * 1024),
        cost_estimate=pl.CostEstimate(flops=0, bytes_accessed=12 * 1024 * 1024, transcendentals=0),
    )(rim, field, before, after, source, earlier)


def residual_kernel(omega_ref, log_ref, prior_ref, rest_ref, field_ref, out_ref, held, sems):
    planes = field_ref.shape[2]
    omega = omega_ref[0]
    conduct = prior_ref[...]
    held_z, held_y = mean_along(conduct, 1), mean_along(conduct, 0)
    copies = []
    for i in range(planes):
        conduct = jnp.exp(log_ref[i])
        mean_z, mean_y = mean_along(conduct, 1), mean_along(conduct, 0)
        sigma = (mean_along(mean_z, 0), 0.5 * (mean_z + held_z), 0.5 * (mean_y + held_y))
        for comp in range(3):
            scaled = omega * sigma[comp]
            held[0, comp, i] = rest_ref[0, comp, i] - scaled * field_ref[1, comp, i]
            held[1, comp, i] = rest_ref[1, comp, i] + scaled * field_ref[0, comp, i]
        held_z, held_y = mean_z, mean_y
        copies.append(pltpu.make_async_copy(held.at[:, :, i], out_ref.at[:, :, i], sems.at[i]))
        copies[-1].start()
    for copy in copies:
        copy.wait()


def residual(omega, log_cond, prior, rest, field):
    vmem = pl.BlockSpec(memory_space=pltpu.VMEM)
    return pl.pallas_call(
        residual_kernel,
        in_specs=[pl.BlockSpec(memory_space=pltpu.SMEM)] + [vmem] * 4,
        out_specs=pl.BlockSpec(memory_space=pl.ANY),
        out_shape=jax.ShapeDtypeStruct(field.shape, jnp.float32),
        scratch_shapes=[
            pltpu.VMEM(field.shape, jnp.float32),
            pltpu.SemaphoreType.DMA((field.shape[2],)),
        ],
        compiler_params=pltpu.CompilerParams(vmem_limit_bytes=16 * 1024 * 1024),
    )(omega, log_cond, prior, rest, field)


def per_device(model, block_owner_rank, source_slot, weights, field, source, freq):
    efield = field[0]
    planes, cells_y = efield.shape[2:4]
    first_device = lax.axis_index(SUB) == 0

    halos = [shifted(efield[:, :, -1:], SUB, 1), shifted(efield[:, :, :1], SUB, -1)]
    log_cond, near = log_conductivity(model, block_owner_rank, source_slot, weights)
    log_cond = log_cond.reshape(planes, cells_y, -1)
    rim = jnp.where(first_device, 0.0, 1.0).astype(jnp.float32)[None]
    rest = curl_less_source(rim, efield, *halos, source[0], near)
    prior = shifted(jnp.exp(log_cond[-1]), SUB, 1)
    prior = jnp.where(first_device, jnp.exp(log_cond[0]), prior)
    return residual(freq, log_cond, prior, rest, efield)[None]


def solution(mesh):
    fine = Mesh(mesh.devices.reshape(4, 8, 4, 2), ("y",) + SUB)
    in_specs = (
        P("y", SUB, None),
        P("y", SUB, None),
        P("y", SUB, None),
        P("y", SUB, None),
        P("y", None, None, SUB, None, None),
        P("y", None, None, SUB, None, None),
        P("y"),
    )
    out_specs = P("y", None, None, SUB, None, None)
    return jax.shard_map(
        per_device, mesh=fine, in_specs=in_specs, out_specs=out_specs, check_vma=False
    )
```

```python
import functools

import jax
import jax.numpy as jnp
from jax import lax
from jax.experimental import pallas as pl
from jax.experimental.pallas import tpu as pltpu
from jax.sharding import Mesh, PartitionSpec as P

CHUNK = 256
FIELDS = 3
STEP = 32
NEAR = 512


def shift_of(count):
    return (count - 1).bit_length()


def lists_kernel(sizes, here_ref, owner_far, slot_far, weight_far, after_ref, out_ref, values, *rest):
    nz, nx, nc, quarter, classes, cap = sizes
    top, columns = owner_far.shape
    owner_ref, slot_ref, weight_ref, sems = rest
    copies = [
        pltpu.make_async_copy(far, near, sems.at[i])
        for i, (far, near) in enumerate(
            ((owner_far, owner_ref), (slot_far, slot_ref), (weight_far, weight_ref))
        )
    ]
    for copy in copies:
        copy.start()
    for copy in copies:
        copy.wait()
    owner, slot, weight = owner_ref[...], slot_ref[...], weight_ref[...]
    bits_c, bits_x, bits_q = shift_of(nc), shift_of(nx), shift_of(quarter)
    kind = (slot >> bits_q) * nx + ((owner >> bits_c) & (nx - 1))
    layer = (((owner >> (bits_c + bits_x)) - here_ref[0]) * (2 * here_ref[1] - 1)) & (nz - 1)
    core = (owner - here_ref[1]) & (nc - 1)
    row = (core * nz + layer) * quarter + (slot & (quarter - 1))
    column = lax.broadcasted_iota(jnp.int32, (top, columns), 1)
    as_float = lambda value: value.astype(jnp.float32)
    rounded = lambda value: value.astype(jnp.bfloat16).astype(jnp.float32)
    high = rounded(weight)
    middle = rounded(weight - high)
    parts = [
        as_float(row >> 7),
        as_float(row & 127),
        as_float(column >> 8),
        as_float(column & 255),
        high,
        middle,
        weight - high - middle,
        jnp.zeros((top, columns), jnp.float32),
    ]
    iota_kind = lax.broadcasted_iota(jnp.int32, (classes, columns), 0)
    marks = []
    for k in range(top):
        mark = iota_kind == kind[k : k + 1, :]
        marks.append(jnp.where(mark, 1.0, 0.0))
        stacked = [jnp.where(mark, part[k : k + 1, :], 0.0) for part in parts]
        values[k] = jnp.concatenate(stacked, 0).astype(jnp.bfloat16)
    marks = jnp.concatenate(marks, 0)
    marks_low = marks.astype(jnp.bfloat16)
    rows = top * classes
    half = columns // 2
    column_i = lax.broadcasted_iota(jnp.int32, (columns, columns), 0)
    column_j = lax.broadcasted_iota(jnp.int32, (columns, columns), 1)
    before = (column_i < column_j) & ((column_i >= half) == (column_j >= half))
    prefix = jnp.dot(
        marks_low,
        jnp.where(before, 1.0, 0.0).astype(jnp.bfloat16),
        preferred_element_type=jnp.float32,
    )
    row_i = lax.broadcasted_iota(jnp.int32, (rows, rows), 0)
    row_j = lax.broadcasted_iota(jnp.int32, (rows, rows), 1)
    earlier = (row_j < row_i) & ((row_i & (classes - 1)) == (row_j & (classes - 1)))
    above = jnp.dot(
        jnp.where(earlier, 1.0, 0.0).astype(jnp.bfloat16),
        marks_low,
        preferred_element_type=jnp.float32,
    )
    over = lambda value: jnp.sum(value, axis=1, keepdims=True)

    def per_kind(value):
        sums = over(value)
        total = sums[:classes]
        for k in range(1, top):
            total = total + sums[k * classes : (k + 1) * classes]
        return total

    count_a, count_b = per_kind(marks[:, :half]), per_kind(marks[:, half:])
    begin_b = ((count_a.astype(jnp.int32) + 127) >> 7) << 7
    most = jnp.max(begin_b + count_b.astype(jnp.int32))
    begin_rows = jnp.concatenate([begin_b.astype(jnp.float32)] * top, 0)
    base_a, base_b = over(above[:, :half]), over(above[:, half:]) + begin_rows
    lanes = lax.broadcasted_iota(jnp.int32, (rows, columns), 1)
    placed = marks * (prefix + jnp.where(lanes < half, base_a, base_b))
    ranks = [
        jnp.sum(placed[k * classes : (k + 1) * classes], axis=0, keepdims=True).astype(jnp.int32)
        for k in range(top)
    ]
    lane_rows = cap // 128
    for f, total in enumerate((count_a, count_b)):
        spread = jnp.broadcast_to(total, (classes, 128))
        for c in range(classes):
            at = FIELDS * lane_rows + f
            out_ref[c, at : at + 1, :] = spread[c : c + 1, :]
    iota_rank = lax.broadcasted_iota(jnp.int32, (CHUNK, columns), 0)

    def one_chunk(j, carry):
        found = jnp.zeros((CHUNK, len(parts) * classes), jnp.float32)
        for k in range(top):
            hot = jnp.where(iota_rank == ranks[k] - j * CHUNK, 1.0, 0.0).astype(jnp.bfloat16)
            found = found + lax.dot_general(
                hot, values[k], (((1,), (1,)), ((), ())), preferred_element_type=jnp.float32
            )
        turned = found.T
        part = lambda p: turned[p * classes : (p + 1) * classes]
        fields = [
            part(0) * 128.0 + part(1),
            part(4) + part(5) + part(6),
            part(2) * 256.0 + part(3),
        ]
        for f in range(FIELDS):
            for h in range(CHUNK // 128):
                at = f * lane_rows + j * (CHUNK // 128) + h
                for c in range(classes):
                    out_ref[c, pl.ds(at, 1), :] = fields[f][c : c + 1, h * 128 : (h + 1) * 128]
        return carry

    lax.fori_loop(0, (most + CHUNK - 1) // CHUNK, one_chunk, 0)


def build_lists(sizes, here, owner, slot, weight, after):
    nz, nx, nc, quarter, classes, cap = sizes
    top, columns = owner.shape
    lane_rows = cap // 128
    return pl.pallas_call(
        functools.partial(lists_kernel, sizes),
        out_shape=jax.ShapeDtypeStruct((classes, -(-(FIELDS * lane_rows + 2) // 8) * 8, 128), jnp.float32),
        in_specs=[pl.BlockSpec(memory_space=pltpu.SMEM)] + [pl.BlockSpec(memory_space=pl.ANY)] * 4,
        out_specs=pl.BlockSpec(memory_space=pltpu.VMEM),
        scratch_shapes=[
            pltpu.VMEM((top, 8 * classes, columns), jnp.bfloat16),
            pltpu.VMEM((top, columns), jnp.int32),
            pltpu.VMEM((top, columns), jnp.int32),
            pltpu.VMEM((top, columns), jnp.float32),
            pltpu.SemaphoreType.DMA((3,)),
        ],
        cost_estimate=pl.CostEstimate(flops=0, bytes_accessed=12 * 1024 * 1024, transcendentals=0),
        compiler_params=pltpu.CompilerParams(vmem_limit_bytes=24 * 1024 * 1024),
    )(here, owner, slot, weight, after)


def partials_kernel(
    jobs, sizes, place_ref, count_ref, row_ref, weight_ref, list_ref, table_ref, *rest
):
    ny, nx, cap = sizes
    outs, picked = rest[-1 - len(jobs) : -1], rest[-1]
    columns = outs[0].shape[1] // 2
    lane_rows = cap // 128
    iota = lax.broadcasted_iota(jnp.int32, (columns, 128), 0)
    lanes = lax.broadcasted_iota(jnp.int32, (1, 128), 1)
    depth = lax.broadcasted_iota(jnp.int32, (CHUNK, 128), 0)

    def gather(slot, at, begin, count, j):
        first = begin + j * CHUNK
        left = jnp.minimum(count - j * CHUNK, CHUNK)
        near = first + CHUNK <= NEAR

        @pl.when(near)
        def _():
            start = at * NEAR + first

            def some(i, carry):
                base = pl.multiple_of(i * STEP, STEP)
                for u in range(STEP):
                    picked[slot, pl.ds(base + u, 1), :] = (
                        table_ref[pl.ds(row_ref[start + base + u], 1), :] * weight_ref[start + base + u]
                    )
                return carry

            lax.fori_loop(0, (left + STEP - 1) // STEP, some, 0)

        @pl.when(jnp.logical_not(near))
        def _():
            def single(u, carry):
                line = lax.shift_right_logical(first + u, 7)
                here = lanes == jnp.bitwise_and(first + u, 127)
                pick = lambda f: jnp.sum(
                    jnp.where(here, list_ref[at, pl.ds(f * lane_rows + line, 1), :], 0.0)
                )
                row = pick(0).astype(jnp.int32)
                picked[slot, pl.ds(u, 1), :] = table_ref[pl.ds(row, 1), :] * pick(1)
                return carry

            lax.fori_loop(0, left, single, 0)

    def combine(slot, half, at, begin, count, j):
        first = begin + j * CHUNK
        left = count - j * CHUNK
        rows = jnp.where(depth < left, picked[slot], 0.0)
        high = rows.astype(jnp.bfloat16)
        low = (rows - high.astype(jnp.float32)).astype(jnp.bfloat16)
        hot = []
        for h in range(CHUNK // 128):
            line = 2 * lane_rows + lax.shift_right_logical(first, 7) + h
            place = list_ref[at, pl.ds(line, 1), :].astype(jnp.int32) - half * columns
            place = jnp.where(lanes < left - h * 128, place, -1)
            hot.append(jnp.where(iota == place, 1.0, 0.0).astype(jnp.bfloat16))
        summed = jnp.dot(
            jnp.concatenate(hot, 1), jnp.concatenate([high, low], 1), preferred_element_type=jnp.float32
        )
        return summed[:, :128] + summed[:, 128:]

    tasks = []
    for (offset, begin_t), out_ref in zip(jobs, outs):
        for step in range(out_ref.shape[0]):
            t, swap = begin_t + step, place_ref[2]
            y = (place_ref[0] + jnp.where(swap == 0, offset, t)) % ny
            x = (place_ref[1] + jnp.where(swap == 0, t, offset)) % nx
            at = y * nx + x
            count_a = count_ref[at]
            begin_b = lax.shift_left(lax.shift_right_logical(count_a + 127, 7), 7)
            tasks.append((out_ref, step, 0, at, 0, count_a))
            tasks.append((out_ref, step, 1, at, begin_b, count_ref[ny * nx + at]))
    for slot, (_, _, _, at, begin, count) in enumerate(tasks):
        gather(slot, at, begin, count, 0)
    for slot, (out_ref, step, half, at, begin, count) in enumerate(tasks):
        out_ref[step, half * columns : (half + 1) * columns, :] = combine(slot, half, at, begin, count, 0)
    for out_ref, step, half, at, begin, count in tasks:

        def more(j, carry):
            gather(0, at, begin, count, j)
            out_ref[step, half * columns : (half + 1) * columns, :] += combine(0, half, at, begin, count, j)
            return carry

        lax.fori_loop(1, (count + CHUNK - 1) // CHUNK, more, 0)


def partial_sums(jobs, sizes, columns, cost, place, counts, near_rows, near_weights, lists, table, after):
    ny, nx, cap = sizes
    vmem = pl.BlockSpec(memory_space=pltpu.VMEM)
    smem = pl.BlockSpec(memory_space=pltpu.SMEM)
    anywhere = pl.BlockSpec(memory_space=pl.ANY)
    return pl.pallas_call(
        functools.partial(partials_kernel, [job[:2] for job in jobs], sizes),
        in_specs=[smem, smem, smem, smem, vmem, vmem] + [anywhere] * len(after),
        out_specs=[vmem] * len(jobs),
        scratch_shapes=[
            pltpu.VMEM((2 * sum(job[2] for job in jobs), CHUNK, 128), jnp.float32),
        ],
        out_shape=[
            jax.ShapeDtypeStruct((job[2], columns, 128), jnp.float32) for job in jobs
        ],
        compiler_params=pltpu.CompilerParams(vmem_limit_bytes=24 * 1024 * 1024),
        cost_estimate=pl.CostEstimate(
            flops=0, bytes_accessed=cost, transcendentals=0
        ),
    )(place, counts, near_rows, near_weights, lists, table, *after)


def moved(value, axis, by):
    count = lax.axis_size(axis)
    return lax.ppermute(value, axis, [(i, (i + by) % count) for i in range(count)])


def ordered(value, *earlier):
    anywhere = pl.BlockSpec(memory_space=pl.ANY)
    return pl.pallas_call(
        lambda *refs: None,
        in_specs=[anywhere] * (1 + len(earlier)),
        out_specs=anywhere,
        out_shape=jax.ShapeDtypeStruct(value.shape, value.dtype),
        input_output_aliases={0: 0},
        compiler_params=pltpu.CompilerParams(vmem_limit_bytes=1024 * 1024),
    )(value, *earlier)


def assemble_kernel(spots, *refs):
    sources, (out_ref, sems) = refs[:-2], refs[-2:]
    copies = [
        pltpu.make_async_copy(
            sources[source].at[pl.ds(begin, size)], out_ref.at[pl.ds(target, size)], sems.at[i]
        )
        for i, (source, begin, size, target) in enumerate(spots)
    ]
    for copy in copies:
        copy.start()
    for copy in copies:
        copy.wait()


def gathered(own, make_lists):
    rows, block = own.shape
    nz, nc = lax.axis_size("z"), lax.axis_size("c")
    onward = [(z * nc, (z + 1) % nz * nc) for z in range(nz)]
    onward += [(z * nc + 1, (z - 1) % nz * nc + 1) for z in range(nz)]
    swapped = lambda value: moved(value, "c", 1)
    mate = swapped(own)
    lists = make_lists(mate)
    arrays, spots = [], []

    def take(array, spot):
        spots.append((len(arrays), 0, array.shape[0], spot * rows))
        arrays.append(array)

    take(own, 0)
    take(mate, nz)
    pair = [own, mate]
    for step in range(1, nz // 2 + 1):
        if step == nz // 2:
            pair = pair[:1]
        pair = [lax.ppermute(one, ("z", "c"), onward) for one in pair]
        if step == 1:
            pair[0] = ordered(pair[0], lists)
        elif step < nz // 2:
            pair[0] = ordered(pair[0], mates, arrays[3 if step == 2 else 5])
        mates = pair[-1]
        for core, one in enumerate(pair):
            take(one, core * nz + step)
            take(swapped(one), (1 - core) * nz + nz - step)
    anywhere = pl.BlockSpec(memory_space=pl.ANY)
    table = pl.pallas_call(
        functools.partial(assemble_kernel, tuple(spots)),
        in_specs=[anywhere] * len(arrays),
        out_specs=pl.BlockSpec(memory_space=pltpu.VMEM),
        scratch_shapes=[pltpu.SemaphoreType.DMA((len(spots),))],
        out_shape=jax.ShapeDtypeStruct((nc * nz * rows, block), own.dtype),
        compiler_params=pltpu.CompilerParams(vmem_limit_bytes=16 * 1024 * 1024),
    )(*arrays)
    return table, lists


def shifted(shard, axis, by):
    devices = lax.axis_size(axis)
    pairs = [(i, i + by) for i in range(devices) if 0 <= i + by < devices]
    return lax.ppermute(shard, axis, pairs)


SUB = ("z", "x", "c")


def log_conductivity(model, block_owner_rank, source_slot, weights):
    ny, nz, nx, nc = (lax.axis_size(a) for a in ("y", "z", "x", "c"))
    quarter, block = model.shape[0], model.shape[2]
    columns, top = weights.shape[1:]
    here = jnp.stack([lax.axis_index("z"), lax.axis_index("c")]).astype(jnp.int32)
    classes = ny * nx
    cap = min(columns * top, nz * nc * 128) + CHUNK
    sizes = (nz, nx, nc, quarter, classes, cap)

    def make_lists(after):
        return build_lists(
            sizes, here, block_owner_rank[0].T, source_slot[0].T, weights[0].T, after
        )

    table, lists = gathered(model.reshape(quarter, block), make_lists)
    lists = lax.all_to_all(lists, ("y", "x"), split_axis=0, concat_axis=0, tiled=True)
    lane_rows, near = cap // 128, NEAR // 128
    near_rows = lists[:, :near].reshape(-1).astype(jnp.int32)
    near_factors = lists[:, lane_rows : lane_rows + near].reshape(-1)
    counts = lists[:, FIELDS * lane_rows : FIELDS * lane_rows + 2, 0].T.reshape(-1).astype(jnp.int32)
    place = jnp.stack([lax.axis_index(a) for a in ("y", "x", "c")]).astype(jnp.int32)

    def sums(after, cost, *offsets):
        return partial_sums(
            offsets, (ny, nx, cap), columns, cost, place, counts, near_rows, near_factors, lists, table, after
        )

    def sent(value, by, turn):
        pairs = []
        for i in range(ny * nx * nc):
            y, x, c = i // (nx * nc), i // nc % nx, i % nc
            to_y, to_x = ((y + by) % ny, x) if c == turn else (y, (x + by) % nx)
            pairs.append((i, (to_y * nx + to_x) * nc + c))
        return lax.ppermute(value, ("y", "x", "c"), pairs)

    mib = 1024 * 1024
    (far,) = sums((), 10 * mib, (2, 0, nx))
    up, down = sums((far,), 40 * mib, (1, 0, nx), (3, 0, nx))
    far = sent(far, 2, 0)
    (near,) = sums((far,), 40 * mib, (0, 0, nx))
    got = [far, sent(up, 1, 0), sent(down, 3, 0)]
    joined = [near[d] + got[0][d] + got[1][d] + got[2][d] for d in range(nx)]
    return sum((sent(joined[d], d, 1) for d in (2, 1, 3)), joined[0]), near


def next_along(value, axis):
    length = value.shape[axis]
    place = lax.broadcasted_iota(jnp.int32, value.shape, axis)
    return jnp.where(place == length - 1, 0.0, pltpu.roll(value, length - 1, axis))


def last_along(value, axis, edge):
    place = lax.broadcasted_iota(jnp.int32, value.shape, axis)
    return jnp.where(place == 0, edge, pltpu.roll(value, 1, axis))


def ahead(value, axis):
    return next_along(value, axis) - value


def behind(value, axis):
    return value - last_along(value, axis, 0.0)


def mean_along(value, axis):
    return 0.5 * (value + last_along(value, axis, value))


def curl_kernel(rim_ref, field_ref, before_ref, after_ref, source_ref, earlier_ref, out_ref):
    planes = field_ref.shape[2]
    rim = rim_ref[0]
    for part in range(2):

        def edges(i):
            ref, at = (before_ref, 0) if i < 0 else (after_ref, 0) if i == planes else (field_ref, i)
            return [ref[part, comp, at] for comp in range(3)]

        now, held_y, held_z = edges(-1), None, None
        for i in range(-1, planes):
            later = edges(i + 1)
            ex, ey, ez = now
            hy = ahead(ex, 1) - (later[2] - ez)
            hz = (later[1] - ey) - ahead(ex, 0)
            if i < 0:
                hy, hz = hy * rim, hz * rim
            else:
                hx = ahead(ez, 0) - ahead(ey, 1)
                curl = (
                    behind(hz, 0) - behind(hy, 1),
                    behind(hx, 1) - (hz - held_z),
                    (hy - held_y) - behind(hx, 0),
                )
                for comp in range(3):
                    out_ref[part, comp, i] = curl[comp] - source_ref[part, comp, i]
            now, held_y, held_z = later, hy, hz


def curl_less_source(rim, field, before, after, source, earlier):
    vmem = pl.BlockSpec(memory_space=pltpu.VMEM)
    return pl.pallas_call(
        curl_kernel,
        in_specs=[pl.BlockSpec(memory_space=pltpu.SMEM)] + [vmem] * 4 + [pl.BlockSpec(memory_space=pl.ANY)],
        out_specs=vmem,
        out_shape=jax.ShapeDtypeStruct(field.shape, jnp.float32),
        compiler_params=pltpu.CompilerParams(vmem_limit_bytes=16 * 1024 * 1024),
        cost_estimate=pl.CostEstimate(flops=0, bytes_accessed=12 * 1024 * 1024, transcendentals=0),
    )(rim, field, before, after, source, earlier)


def residual_kernel(omega_ref, log_ref, prior_ref, rest_ref, field_ref, out_ref, held, sems):
    planes = field_ref.shape[2]
    omega = omega_ref[0]
    conduct = prior_ref[...]
    held_z, held_y = mean_along(conduct, 1), mean_along(conduct, 0)
    copies = []
    for i in range(planes):
        conduct = jnp.exp(log_ref[i])
        mean_z, mean_y = mean_along(conduct, 1), mean_along(conduct, 0)
        sigma = (mean_along(mean_z, 0), 0.5 * (mean_z + held_z), 0.5 * (mean_y + held_y))
        for comp in range(3):
            scaled = omega * sigma[comp]
            held[0, comp, i] = rest_ref[0, comp, i] - scaled * field_ref[1, comp, i]
            held[1, comp, i] = rest_ref[1, comp, i] + scaled * field_ref[0, comp, i]
        held_z, held_y = mean_z, mean_y
        copies.append(pltpu.make_async_copy(held.at[:, :, i], out_ref.at[:, :, i], sems.at[i]))
        copies[-1].start()
    for copy in copies:
        copy.wait()


def residual(omega, log_cond, prior, rest, field):
    vmem = pl.BlockSpec(memory_space=pltpu.VMEM)
    return pl.pallas_call(
        residual_kernel,
        in_specs=[pl.BlockSpec(memory_space=pltpu.SMEM)] + [vmem] * 4,
        out_specs=pl.BlockSpec(memory_space=pl.ANY),
        out_shape=jax.ShapeDtypeStruct(field.shape, jnp.float32),
        scratch_shapes=[
            pltpu.VMEM(field.shape, jnp.float32),
            pltpu.SemaphoreType.DMA((field.shape[2],)),
        ],
        compiler_params=pltpu.CompilerParams(vmem_limit_bytes=16 * 1024 * 1024),
    )(omega, log_cond, prior, rest, field)


def per_device(model, block_owner_rank, source_slot, weights, field, source, freq):
    efield = field[0]
    planes, cells_y = efield.shape[2:4]
    first_device = lax.axis_index(SUB) == 0

    halos = [shifted(efield[:, :, -1:], SUB, 1), shifted(efield[:, :, :1], SUB, -1)]
    log_cond, near = log_conductivity(model, block_owner_rank, source_slot, weights)
    log_cond = log_cond.reshape(planes, cells_y, -1)
    rim = jnp.where(first_device, 0.0, 1.0).astype(jnp.float32)[None]
    rest = curl_less_source(rim, efield, *halos, source[0], near)
    prior = shifted(jnp.exp(log_cond[-1]), SUB, 1)
    prior = jnp.where(first_device, jnp.exp(log_cond[0]), prior)
    return residual(freq, log_cond, prior, rest, efield)[None]


def solution(mesh):
    fine = Mesh(mesh.devices.reshape(4, 8, 4, 2), ("y",) + SUB)
    in_specs = (
        P("y", SUB, None),
        P("y", SUB, None),
        P("y", SUB, None),
        P("y", SUB, None),
        P("y", None, None, SUB, None, None),
        P("y", None, None, SUB, None, None),
        P("y"),
    )
    out_specs = P("y", None, None, SUB, None, None)
    return jax.shard_map(
        per_device, mesh=fine, in_specs=in_specs, out_specs=out_specs, check_vma=False
    )
```
